512 devices in a mesh: section: 32 (over z, x), tensor: 16 (over y, core).
Axes of the slice: x: 4, y: 8, z: 8, core: 2. Of those that a mesh axis runs over, the one named last changes fastest.
Arguments:
- hidden_rows: bfloat16 [32, 2, 8192], P('section', None, 'tensor'), may hold values from -10 to 10
- entering_rows: bfloat16 [3, 2, 8192], P(None, None, 'tensor'), may hold values from -10 to 10
- norm_gain: bfloat16 [32, 8192], P('section', 'tensor'), may hold values from 0.099609375 to 1.8984375
- key_weight: bfloat16 [32, 8192, 512], P('section', 'tensor'), may hold values from -0.0625 to 0.0625
- value_weight: bfloat16 [32, 8192, 512], P('section', 'tensor'), may hold values from -0.0625 to 0.0625
- queries: bfloat16 [32, 4, 2, 8192], P('section'), may hold values from -8 to 8
- cache_keys: bfloat16 [32, 4, 2, 2048, 512], P('section', None, None, 'tensor'), may hold values from -50 to 50
- cache_values: bfloat16 [32, 4, 2, 2048, 512], P('section', None, None, 'tensor'), may hold values from -5 to 5
- lengths: int32 [4, 2], replicated, may hold values from 2 to 2048, as said below
- plan: int32 [4], replicated, may hold values from 0 to 3, each once
Outputs:
- processed_rows: bfloat16 [32, 2, 8192], P('section', None, 'tensor')
The draws below stay inside these ranges and needn't reach their ends.
Inputs may be any that keep to these rules, and one draw needn't show every extreme that they name: `lengths`: every request has at least 2 cached positions, and in every draw some request has all 2048.
All inputs are finite; a program needn't handle non-finite values.
Results may differ from the reference program's by a relative error of at most 0.015.
Values may be sent and summed in bfloat16 or wider, within the bound.
A program may use at most 64 MiB of HBM per device.

```python
import jax
import jax.numpy as jnp
from jax import lax

D = 8192
HQ = 64
KVH = 4
HD = 128
MB = 4
REQS = 2
SECTIONS = 32
CTX = 2048


def query_laws(key):
    shape_all = (SECTIONS, MB, REQS, HQ * HD)
    drawn_draw = jnp.clip(jax.random.normal(jax.random.fold_in(key, 101), shape_all, jnp.float32), -4.0, 4.0) * 1.5
    return drawn_draw


def stretched_rows(key, shape_all, low_scale, rise_factor):
    columns = jnp.arange(shape_all[-1], dtype=jnp.float32) / shape_all[-1]
    jitter = jnp.exp(jax.random.uniform(jax.random.fold_in(key, 1), (shape_all[-1],), jnp.float32, -0.5, 0.5))
    col_scale = low_scale * rise_factor ** columns * jitter
    normal_part = jnp.clip(jax.random.normal(jax.random.fold_in(key, 2), shape_all, jnp.float32), -3.5, 3.5)
    return normal_part * col_scale


def draw_hidden_rows(key, part):
    key = jax.random.fold_in(key, 11)
    return stretched_rows(key, (SECTIONS, REQS, D), 0.5, 3.0).astype(jnp.bfloat16)


def draw_entering_rows(key, part):
    key = jax.random.fold_in(key, 13)
    return stretched_rows(key, (MB - 1, REQS, D), 0.5, 3.0).astype(jnp.bfloat16)


def draw_queries(key, part):
    drawn_draw = query_laws(key)
    return drawn_draw.astype(jnp.bfloat16)


def draw_cache_keys(key, part):
    key = jax.random.fold_in(key, 23)
    shape_all = (SECTIONS, MB, REQS, CTX, KVH, HD)
    key_rows = jnp.clip(jax.random.normal(jax.random.fold_in(key, 1), shape_all, jnp.float32), -5.0, 5.0)
    return key_rows.reshape(SECTIONS, MB, REQS, CTX, KVH * HD).astype(jnp.bfloat16)


def draw_lengths(key, part):
    key = jax.random.fold_in(key, 31)
    raw_len = jax.random.randint(jax.random.fold_in(key, 1), (MB, REQS), 2, CTX + 1)
    shift_bits = jax.random.randint(jax.random.fold_in(key, 2), (MB, REQS), 0, 8)
    short_len = jnp.maximum(jnp.right_shift(raw_len, shift_bits), 2)
    longest = jax.random.randint(jax.random.fold_in(key, 3), (), 0, MB * REQS)
    flat_len = jnp.where(jnp.arange(MB * REQS) == longest, CTX, short_len.reshape(-1))
    return flat_len.reshape(MB, REQS).astype(jnp.int32)


def levels(own_key, extent, split, smallest, largest):
    level = 1.0
    for dim, blocks in split:
        heights = jax.random.uniform(jax.random.fold_in(jax.random.fold_in(own_key, 6), dim), (blocks,), jnp.float32, smallest / len(split), largest / len(split))
        level = level * jnp.repeat(jnp.exp(heights), extent[dim] // blocks).reshape((-1,) + (1,) * (len(extent) - 1 - dim))
    return level


def noise(stream_key, extent, scale, limit, cuts=(), kind=jnp.bfloat16):
    level = levels(stream_key, extent, cuts, -0.22, 0.18) if cuts else 1.0
    result = jax.random.normal(stream_key, extent, jnp.float32) * scale * level
    return jnp.minimum(jnp.maximum(result, -limit), limit).astype(kind)


def setup_inputs(seed: int = 0) -> dict:
    key_of = jax.random.split(jax.random.key(seed), 11)
    hidden_rows = draw_hidden_rows(jax.random.fold_in(key_of[10], 71), 0)
    entering_rows = draw_entering_rows(jax.random.fold_in(key_of[10], 71), 0)
    norm_gain = jnp.clip(1.0 + 0.18 * jax.random.normal(key_of[2], (SECTIONS, D), jnp.float32), 0.099609375, 1.8984375).astype(jnp.bfloat16)
    key_weight = noise(key_of[3], (SECTIONS, D, KVH * HD), D ** -0.5, 0.0625, ((0, 32), (1, 16)))
    value_weight = noise(key_of[4], (SECTIONS, D, KVH * HD), D ** -0.5, 0.0625, ((0, 32), (1, 16)))
    queries = draw_queries(jax.random.fold_in(key_of[10], 71), 0)
    cache_keys = draw_cache_keys(jax.random.fold_in(key_of[10], 71), 0)
    cache_values = noise(key_of[7], (SECTIONS, MB, REQS, CTX, KVH * HD), 1.0, 5.0, ((0, 32), (3, 16)))
    lengths = draw_lengths(jax.random.fold_in(key_of[10], 71), 0)
    plan = jax.random.permutation(key_of[9], MB).astype(jnp.int32)
    return {"hidden_rows": hidden_rows, "entering_rows": entering_rows, "norm_gain": norm_gain, "key_weight": key_weight, "value_weight": value_weight, "queries": queries, "cache_keys": cache_keys, "cache_values": cache_values, "lengths": lengths, "plan": plan}


epsilon = 1e-05

def rounded(values):
    return lax.optimization_barrier(values.astype(jnp.bfloat16)).astype(jnp.float32)

def rotate_keys(key_rows, position):
    half_dim = key_rows.shape[-1] // 2
    freq_rates = jnp.exp(jnp.arange(half_dim, dtype=jnp.float32) * (-2.0 * jnp.log(500000.0) / key_rows.shape[-1]))
    angle_row = position.astype(jnp.float32)[:, None] * freq_rates[None, :]
    cosine = jnp.cos(angle_row)[:, None, :]
    sine_part = jnp.sin(angle_row)[:, None, :]
    first_half = key_rows[..., :half_dim]
    second_half = key_rows[..., half_dim:]
    return jnp.concatenate([first_half * cosine - second_half * sine_part, second_half * cosine + first_half * sine_part], axis=-1)

def apply_layer(rows, gain_row, key_matrix, value_matrix, query_rows, key_block, value_block, length):
    req_count = rows.shape[0]
    group_size = HQ // KVH
    wide_rows = rows.astype(jnp.float32)
    mean_sq = lax.optimization_barrier(jnp.mean(wide_rows * wide_rows, axis=1, keepdims=True))
    scaled = (wide_rows * gain_row.astype(jnp.float32)).astype(jnp.bfloat16)
    inverse = lax.rsqrt(mean_sq + epsilon)
    key_raw = jnp.dot(scaled, key_matrix, preferred_element_type=jnp.float32) * inverse
    value_raw = jnp.dot(scaled, value_matrix, preferred_element_type=jnp.float32) * inverse
    new_key = rounded(rotate_keys(key_raw.reshape(req_count, KVH, HD), length))
    new_value = rounded(value_raw.reshape(req_count, KVH, HD))
    query_all = query_rows.reshape(req_count, KVH, group_size, HD).astype(jnp.float32)
    key_all = key_block.reshape(req_count, CTX, KVH, HD).astype(jnp.float32)
    value_all = value_block.reshape(req_count, CTX, KVH, HD).astype(jnp.float32)
    scale_qk = HD ** (-0.5)
    scores = jnp.einsum('rkgd,rpkd->rkgp', query_all, key_all, precision=lax.Precision.HIGHEST) * scale_qk
    valid_mask = (jnp.arange(CTX, dtype=jnp.int32)[None, :] < length[:, None])[:, None, None, :]
    own_score = jnp.einsum('rkgd,rkd->rkg', query_all, new_key, precision=lax.Precision.HIGHEST) * scale_qk
    row_top = jnp.maximum(lax.optimization_barrier(jnp.max(jnp.where(valid_mask, scores, -jnp.inf), axis=-1)), own_score)
    weights = rounded(jnp.where(valid_mask, jnp.exp(scores - row_top[..., None]), 0.0))
    own_weight = jnp.exp(own_score - row_top)
    row_total = lax.optimization_barrier(jnp.sum(weights, axis=-1)) + own_weight
    mixed_sum = jnp.einsum('rkgp,rpkd->rkgd', weights, value_all, precision=lax.Precision.HIGHEST)
    mixed_sum = mixed_sum + own_weight[..., None] * new_value[:, :, None, :]
    attention = (mixed_sum / row_total[..., None]).reshape(req_count, HQ * HD)
    return (wide_rows + attention).astype(jnp.bfloat16)

def reference(hidden_rows, entering_rows, norm_gain, key_weight, value_weight, queries, cache_keys, cache_values, lengths, plan):
    state_rows = hidden_rows
    section_ids = jnp.arange(SECTIONS, dtype=jnp.int32)
    for tick_index in range(MB):
        if tick_index > 0:
            state_rows = jnp.concatenate([entering_rows[tick_index - 1][None], state_rows[:-1]], axis=0)
        served = plan[(section_ids - tick_index) % MB]

        def section_layer(section_id):
            batch_id = served[section_id]
            return apply_layer(state_rows[section_id], norm_gain[section_id], key_weight[section_id], value_weight[section_id], queries[section_id, batch_id], cache_keys[section_id, batch_id], cache_values[section_id, batch_id], lengths[batch_id])
        state_rows = lax.map(section_layer, section_ids)
    return state_rows
```

```python
import functools

import jax
import jax.numpy as jnp
from jax import lax
from jax.experimental import pallas as pl
from jax.experimental.pallas import tpu as pltpu
from jax.sharding import PartitionSpec as P

D = 8192
HQ = 64
KVH = 4
HD = 128
TICKS = 4
TENSOR = 16
EPSILON = 1e-05
NEG_BIG = -1e30
MESH = pl.DeviceIdType.MESH
f32 = jnp.float32
bf16 = jnp.bfloat16


def iota(shape, axis):
    return lax.broadcasted_iota(jnp.int32, shape, axis)


def block_diagonal(columns):
    group = iota((HD, HD), 1) // 32
    return jnp.concatenate(
        [jnp.where(group == k, columns, 0.0) for k in range(KVH)], axis=0
    ).astype(bf16)


def kernel(
    hidden_ref,
    entering_ref,
    gain_ref,
    kw_hbm,
    vw_hbm,
    q_hbm,
    ck_hbm,
    cv_hbm,
    len_ref,
    plan_ref,
    out_ref,
    kw,
    vw,
    qv,
    ck,
    cv,
    qs,
    folded,
    part_out,
    part_in,
    stat_out,
    stat_in,
    row_out,
    row_in,
    load_sem,
    part_send,
    part_recv,
    stat_send,
    stat_recv,
    row_send,
    row_recv,
):
    sections = lax.axis_size("section")
    sec = lax.axis_index("section")
    ten = lax.axis_index("tensor")
    following = lax.rem(sec + 1, sections)
    previous = lax.rem(sec + sections - 1, sections)

    loads = [
        pltpu.make_async_copy(src, dst, load_sem.at[i])
        for i, (src, dst) in enumerate(
            [
                (q_hbm.at[0], qv),
                (kw_hbm.at[0], kw),
                (vw_hbm.at[0], vw),
                (ck_hbm.at[0], ck),
                (cv_hbm.at[0], cv),
            ]
        )
    ]
    for load in loads:
        load.start()

    barrier = pltpu.get_barrier_semaphore()
    for k in range(TENSOR):
        pl.semaphore_signal(barrier, inc=1, device_id=(previous, k), device_id_type=MESH)

    slots = [plan_ref[lax.rem(sec + TICKS - j, TICKS)] for j in range(TICKS)]
    spans = [[len_ref[r, slots[j]] for r in range(2)] for j in range(TICKS)]

    row8 = iota((8, HD), 0)
    lane8 = iota((8, HD), 1)
    even_row = row8 % 2 == 0
    lane1 = iota((1, HD), 1)
    even_lane = lane1 % 2 == 0
    mine = lane8 == row8 + ten * 8

    def heads_of(block):
        return jnp.concatenate([block[:, h * HD : (h + 1) * HD] for h in range(4)], axis=0)

    def features_of(block):
        return jnp.concatenate([block[2 * h : 2 * h + 2, :] for h in range(4)], axis=1)

    gain2 = jnp.broadcast_to(gain_ref[...].astype(f32), (2, 512))
    gain8 = heads_of(gain2)

    angle_rows = jnp.zeros((8, HD), f32)
    for j in range(TICKS):
        for r in range(2):
            angle_rows = jnp.where(row8 == 2 * j + r, spans[j][r].astype(f32), angle_rows)
    rates = jnp.exp((lane8 % 64).astype(f32) * (-2.0 * jnp.log(f32(500000.0)) / HD))
    angle = angle_rows * rates
    cosines = jnp.cos(angle)
    sines = jnp.sin(angle)
    sines = jnp.where(lane8 < 64, sines, -sines)

    def query_columns(j):
        rows = qv[slots[j]].astype(f32)
        for h in range(HQ):
            qs[2 * h : 2 * h + 2, :] = rows[:, h * HD : (h + 1) * HD]
        q = qs[...]
        cos8 = jnp.concatenate([cosines[2 * j : 2 * j + 2]] * 4, axis=0)
        sin8 = jnp.concatenate([sines[2 * j : 2 * j + 2]] * 4, axis=0)
        other = pltpu.roll(q, 64, 1)
        turned = (
            q.reshape(16, 8, HD) * cos8[None] + other.reshape(16, 8, HD) * sin8[None]
        ).reshape(HD, HD)
        return block_diagonal(q.T), block_diagonal(turned.T)

    def fold(j, turned):
        folded[j] = jnp.dot(kw[...], turned, preferred_element_type=f32).astype(bf16)

    def stats(j, columns):
        keys = ck[slots[j]].reshape(256, 512)
        both = jnp.dot(keys, columns, preferred_element_type=f32)
        scores = jnp.where(even_lane, both[:HD], both[HD:]) * HD ** (-0.5)
        span = jnp.where(even_lane, spans[j][0], spans[j][1])
        valid = iota((HD, HD), 0) + ten * HD < span
        scores = jnp.where(valid, scores, NEG_BIG)
        top = jnp.max(scores, axis=0, keepdims=True).astype(bf16).astype(f32)
        weights = jnp.where(valid, jnp.exp(scores - top), 0.0).astype(bf16).astype(f32)
        total = jnp.sum(weights, axis=0, keepdims=True)
        turned = weights.T
        even = iota((HD, HD), 0) % 2 == 0
        wide = jnp.concatenate(
            [jnp.where(even, turned, 0.0), jnp.where(even, 0.0, turned)], axis=1
        ).astype(bf16)
        values = cv[slots[j]].reshape(256, 512)
        high = total.astype(bf16).astype(f32)
        extra = jnp.where(
            row8 == 0, top, jnp.where(row8 == 1, high, jnp.where(row8 == 2, total - high, 0.0))
        )
        for k in range(KVH):
            mixed = jnp.dot(
                wide[32 * k : 32 * k + 32],
                values[:, HD * k : HD * k + HD],
                preferred_element_type=f32,
            )
            for i in range(4):
                stat_out[j, 4 * k + i] = jnp.concatenate(
                    [mixed[8 * i : 8 * i + 8], extra], axis=0
                ).astype(bf16)
        if j < TICKS - 1:
            for k in range(TENSOR):
                to = lax.rem(ten + k, TENSOR)
                pltpu.make_async_remote_copy(
                    stat_out.at[j, to],
                    stat_in.at[j, ten],
                    stat_send.at[j],
                    stat_recv.at[j],
                    device_id=(following, to),
                    device_id_type=MESH,
                ).start()
        else:
            for k in range(1, TENSOR):
                to = lax.rem(ten + k, TENSOR)
                pltpu.make_async_remote_copy(
                    stat_out.at[j, to],
                    stat_in.at[j, ten],
                    stat_send.at[j],
                    stat_recv.at[j],
                    device_id=(sec, to),
                    device_id_type=MESH,
                ).start()
            stat_in[j, ten] = stat_out[j, ten]

    def wait_bytes(ref, sem):
        pltpu.make_async_copy(ref, ref, sem).wait()

    def arrived(ref, j):
        return ref.at[j] if j < TICKS - 1 else ref.at[j, pl.ds(0, TENSOR - 1)]

    def merge(j):
        wait_bytes(arrived(stat_in, j), stat_recv.at[j])
        pages = stat_in[j].astype(f32)
        mixed = pages[:, 0:8, :]
        tops = pages[:, 8:9, :]
        totals = pages[:, 9:10, :] + pages[:, 10:11, :]
        top = jnp.max(tops, axis=0, keepdims=True)
        scale = jnp.exp(tops - top)
        total = jnp.sum(scale * totals, axis=0, keepdims=True)
        share = scale / total
        column = jnp.sum(jnp.where(mine[None], share, 0.0), axis=2, keepdims=True)
        mean = jnp.sum(column * mixed, axis=0)
        return mean, (top + jnp.log(total))[0]

    def combine(j, rows, merged):
        mean, level = merged
        wait_bytes(arrived(part_in, j), part_recv.at[j])
        sums = jnp.sum(part_in[j], axis=0)
        mean_sq = sums[3:4] / D + EPSILON
        own = sums[2:3] * lax.rsqrt(mean_sq * HD)
        share = 1.0 / (1.0 + jnp.exp(level - own))
        inverse = lax.rsqrt(mean_sq)
        share_col = jnp.sum(jnp.where(mine, share, 0.0), axis=1, keepdims=True)
        inverse_col = jnp.sum(jnp.where(mine, inverse, 0.0), axis=1, keepdims=True)
        fresh = jnp.where(even_row, sums[0:1], sums[1:2]) * inverse_col
        return (rows + (mean + share_col * (fresh - mean))).astype(bf16).astype(f32)

    def project(j, rows):
        scaled = features_of(rows * gain8).astype(bf16)
        value_part = jnp.dot(scaled, vw[...], preferred_element_type=f32)
        own_part = jnp.dot(scaled, folded[j], preferred_element_type=f32)
        own_row = jnp.where(even_lane, own_part[0:1], own_part[1:2])
        square = rows * rows
        square = square[0:2] + square[2:4] + square[4:6] + square[6:8]
        square = jnp.sum(square, axis=1, keepdims=True)
        square_row = jnp.where(even_lane, square[0:1], square[1:2])
        tail = jnp.concatenate([own_row, square_row], axis=0)
        for k in range(KVH):
            part_out[j, k] = jnp.concatenate(
                [value_part[:, HD * k : HD * k + HD], tail], axis=0
            )

    def send_parts(j):
        for k in range(TENSOR):
            if j == TICKS - 1 and k == 0:
                continue
            to = lax.rem(ten + k, TENSOR)
            pltpu.make_async_remote_copy(
                part_out.at[j, to // 4],
                part_in.at[j, ten],
                part_send.at[j],
                part_recv.at[j],
                device_id=(following if j < TICKS - 1 else sec, to),
                device_id_type=MESH,
            ).start()
        if j == TICKS - 1:
            part_in[j, ten] = part_out[j, ten // 4]

    def row_copy(j):
        return pltpu.make_async_remote_copy(
            row_out.at[j],
            row_in.at[j],
            row_send.at[j],
            row_recv.at[j],
            device_id=(following, ten),
            device_id_type=MESH,
        )

    def send_rows(j, rows):
        row_out[j] = rows
        row_copy(j).start()

    rows = heads_of(hidden_ref[0].astype(f32))
    loads[0].wait()
    columns, turned = query_columns(0)
    loads[1].wait()
    fold(0, turned)
    loads[2].wait()
    project(0, rows)
    pl.semaphore_wait(barrier, TENSOR)
    send_parts(0)
    send_rows(0, rows)
    loads[3].wait()
    loads[4].wait()
    stats(0, columns)
    columns, turned = query_columns(1)
    fold(1, turned)
    stats(1, columns)
    for j in range(1, TICKS):
        row_copy(j - 1).wait_recv()
        merged = merge(j - 1)
        fresh = combine(j - 1, row_in[j - 1], merged)
        rows = jnp.where(sec == 0, heads_of(entering_ref[j - 1].astype(f32)), fresh)
        project(j, rows)
        send_parts(j)
        if j < TICKS - 1:
            send_rows(j, rows)
            columns, turned = query_columns(j + 1)
            fold(j + 1, turned)
            stats(j + 1, columns)
    merged = merge(TICKS - 1)
    final = combine(TICKS - 1, rows, merged)
    out_ref[0] = features_of(final).astype(bf16)

    for j in range(TICKS):
        wait_bytes(arrived(part_in, j), part_send.at[j])
        wait_bytes(arrived(stat_in, j), stat_send.at[j])
        if j < TICKS - 1:
            row_copy(j).wait_send()


def on_device(
    hidden_rows,
    entering_rows,
    norm_gain,
    key_weight,
    value_weight,
    queries,
    cache_keys,
    cache_values,
    lengths,
    plan,
):
    vmem = pl.BlockSpec(memory_space=pltpu.VMEM)
    smem = pl.BlockSpec(memory_space=pltpu.SMEM)
    anywhere = pl.BlockSpec(memory_space=pl.ANY)
    dma = pltpu.SemaphoreType.DMA
    return pl.pallas_call(
        kernel,
        out_shape=jax.ShapeDtypeStruct((1, 2, 512), bf16),
        in_specs=[vmem, vmem, vmem] + [anywhere] * 5 + [smem, smem],
        out_specs=vmem,
        scratch_shapes=[
            pltpu.VMEM((512, 512), bf16),
            pltpu.VMEM((512, 512), bf16),
            pltpu.VMEM((4, 2, 8192), bf16),
            pltpu.VMEM((4, 2, 128, 512), bf16),
            pltpu.VMEM((4, 2, 128, 512), bf16),
            pltpu.VMEM((128, 128), f32),
            pltpu.VMEM((TICKS, 512, 128), bf16),
            pltpu.VMEM((TICKS, KVH, 4, 128), f32),
            pltpu.VMEM((TICKS, TENSOR, 4, 128), f32),
            pltpu.VMEM((TICKS, TENSOR, 16, 128), bf16),
            pltpu.VMEM((TICKS, TENSOR, 16, 128), bf16),
            pltpu.VMEM((TICKS - 1, 8, 128), f32),
            pltpu.VMEM((TICKS - 1, 8, 128), f32),
            dma((5,)),
            dma((TICKS,)),
            dma((TICKS,)),
            dma((TICKS,)),
            dma((TICKS,)),
            dma((TICKS - 1,)),
            dma((TICKS - 1,)),
        ],
        compiler_params=pltpu.CompilerParams(
            collective_id=0, has_side_effects=True, vmem_limit_bytes=60 * 1024 * 1024
        ),
    )(
        hidden_rows,
        entering_rows,
        norm_gain,
        key_weight,
        value_weight,
        queries,
        cache_keys,
        cache_values,
        lengths.T,
        plan,
    )


def solution(mesh):
    in_specs = (
        P("section", None, "tensor"),
        P(None, None, "tensor"),
        P("section", "tensor"),
        P("section", "tensor", None),
        P("section", "tensor", None),
        P("section", None, None, None),
        P("section", None, None, "tensor", None),
        P("section", None, None, "tensor", None),
        P(),
        P(),
    )
    out_specs = P("section", None, "tensor")
    return jax.shard_map(
        on_device, mesh=mesh, in_specs=in_specs, out_specs=out_specs, check_vma=False
    )
```

```python
import functools

import jax
import jax.numpy as jnp
from jax import lax
from jax.experimental import pallas as pl
from jax.experimental.pallas import tpu as pltpu
from jax.sharding import PartitionSpec as P

D = 8192
HQ = 64
KVH = 4
HD = 128
TICKS = 4
TENSOR = 16
EPSILON = 1e-05
NEG_BIG = -1e30
MESH = pl.DeviceIdType.MESH
f32 = jnp.float32
bf16 = jnp.bfloat16


def iota(shape, axis):
    return lax.broadcasted_iota(jnp.int32, shape, axis)


def block_diagonal(columns):
    group = iota((HD, HD), 1) // 32
    return jnp.concatenate(
        [jnp.where(group == k, columns, 0.0) for k in range(KVH)], axis=0
    ).astype(bf16)


def kernel(
    hidden_hbm,
    entering_hbm,
    gain_hbm,
    kw_hbm,
    vw_hbm,
    q_hbm,
    ck_hbm,
    cv_hbm,
    len_hbm,
    plan_hbm,
    out_ref,
    len_ref,
    plan_ref,
    hidden_ref,
    entering_ref,
    gain_ref,
    kw,
    vw,
    qv,
    ck,
    cv,
    qs,
    folded,
    part_out,
    part_in,
    stat_out,
    stat_in,
    row_out,
    row_in,
    load_sem,
    part_send,
    part_recv,
    stat_send,
    stat_recv,
    row_send,
    row_recv,
):
    sections = lax.axis_size("section")
    sec = lax.axis_index("section")
    ten = lax.axis_index("tensor")
    following = lax.rem(sec + 1, sections)
    previous = lax.rem(sec + sections - 1, sections)

    load = {}
    for i, (name, src, dst) in enumerate(
        [
            ("plan", plan_hbm, plan_ref),
            ("len", len_hbm, len_ref),
            ("q", q_hbm.at[0], qv),
            ("hidden", hidden_hbm.at[0], hidden_ref),
            ("gain", gain_hbm, gain_ref),
            ("kw", kw_hbm.at[0], kw),
            ("ck", ck_hbm.at[0], ck),
            ("vw", vw_hbm.at[0], vw),
            ("cv", cv_hbm.at[0], cv),
            ("entering", entering_hbm, entering_ref),
        ]
    ):
        load[name] = pltpu.make_async_copy(src, dst, load_sem.at[i])
        load[name].start()

    first = sec == 0
    last = sec == sections - 1
    chip = ten // 2 * 2
    partner = chip + 1 - lax.rem(ten, 2)
    others = [lax.rem(chip + m, TENSOR) for m in (8, 9, 6, 7, 10, 11, 4, 5, 12, 13, 2, 3, 14, 15)]

    barrier = pltpu.get_barrier_semaphore()

    @pl.when(jnp.logical_not(first))
    def _():
        for k in others + [partner, ten]:
            pl.semaphore_signal(barrier, inc=1, device_id=(previous, k), device_id_type=MESH)

    @pl.when(first)
    def _():
        for k in others + [partner]:
            pl.semaphore_signal(barrier, inc=1, device_id=(sec, k), device_id_type=MESH)

    load["plan"].wait()
    load["len"].wait()
    slots = [plan_ref[lax.rem(sec + TICKS - j, TICKS)] for j in range(TICKS)]
    spans = [[len_ref[r, slots[j]] for r in range(2)] for j in range(TICKS)]

    row8 = iota((8, HD), 0)
    lane8 = iota((8, HD), 1)
    even_row = row8 % 2 == 0
    lane1 = iota((1, HD), 1)
    even_lane = lane1 % 2 == 0
    mine = lane8 == row8 + ten * 8

    def heads_of(block):
        return jnp.concatenate([block[:, h * HD : (h + 1) * HD] for h in range(4)], axis=0)

    def features_of(block):
        return jnp.concatenate([block[2 * h : 2 * h + 2, :] for h in range(4)], axis=1)

    angle_rows = jnp.zeros((8, HD), f32)
    for j in range(TICKS):
        for r in range(2):
            angle_rows = jnp.where(row8 == 2 * j + r, spans[j][r].astype(f32), angle_rows)
    rates = jnp.exp((lane8 % 64).astype(f32) * (-2.0 * jnp.log(f32(500000.0)) / HD))
    angle = angle_rows * rates
    cosines = jnp.cos(angle)
    sines = jnp.sin(angle)
    sines = jnp.where(lane8 < 64, sines, -sines)

    def query_columns(j):
        rows = qv[slots[j]].astype(f32)
        for h in range(HQ):
            qs[2 * h : 2 * h + 2, :] = rows[:, h * HD : (h + 1) * HD]
        q = qs[...]
        cos8 = jnp.concatenate([cosines[2 * j : 2 * j + 2]] * 4, axis=0)
        sin8 = jnp.concatenate([sines[2 * j : 2 * j + 2]] * 4, axis=0)
        other = pltpu.roll(q, 64, 1)
        turned = (
            q.reshape(16, 8, HD) * cos8[None] + other.reshape(16, 8, HD) * sin8[None]
        ).reshape(HD, HD)
        return block_diagonal(q.T), block_diagonal(turned.T)

    def fold(j, turned):
        folded[j] = jnp.dot(kw[...], turned, preferred_element_type=f32).astype(bf16)

    def stats(j, columns):
        keys = ck[slots[j]].reshape(256, 512)
        both = jnp.dot(keys, columns, preferred_element_type=f32)
        scores = jnp.where(even_lane, both[:HD], both[HD:]) * HD ** (-0.5)
        span = jnp.where(even_lane, spans[j][0], spans[j][1])
        valid = iota((HD, HD), 0) + ten * HD < span
        scores = jnp.where(valid, scores, NEG_BIG)
        top = jnp.max(scores, axis=0, keepdims=True).astype(bf16).astype(f32)
        weights = jnp.where(valid, jnp.exp(scores - top), 0.0).astype(bf16).astype(f32)
        total = jnp.sum(weights, axis=0, keepdims=True)
        turned = weights.T
        even = iota((HD, HD), 0) % 2 == 0
        wide = jnp.concatenate(
            [jnp.where(even, turned, 0.0), jnp.where(even, 0.0, turned)], axis=1
        ).astype(bf16)
        values = cv[slots[j]].reshape(256, 512)
        high = total.astype(bf16).astype(f32)
        extra = jnp.where(
            row8 == 0, top, jnp.where(row8 == 1, high, jnp.where(row8 == 2, total - high, 0.0))
        )
        for k in range(KVH):
            mixed = jnp.dot(
                wide[32 * k : 32 * k + 32],
                values[:, HD * k : HD * k + HD],
                preferred_element_type=f32,
            )
            for i in range(4):
                stat_out[j, 4 * k + i] = jnp.concatenate(
                    [mixed[8 * i : 8 * i + 8], extra], axis=0
                ).astype(bf16)

    def send_page(source, target, j, send, receive):
        def to_section(section, partners):
            for to in partners:
                pltpu.make_async_remote_copy(
                    source(to),
                    target.at[j, ten],
                    send.at[j],
                    receive.at[j],
                    device_id=(section, to),
                    device_id_type=MESH,
                ).start()

        if j < TICKS - 1:

            @pl.when(jnp.logical_not(last))
            def _():
                to_section(following, others + [partner, ten])
        else:
            to_section(sec, others + [partner])

    def send_stats(j):
        send_page(lambda to: stat_out.at[j, to], stat_in, j, stat_send, stat_recv)
        if j == TICKS - 1:
            stat_in[j, ten] = stat_out[j, ten]

    def wait_bytes(ref, sem):
        pltpu.make_async_copy(ref, ref, sem).wait()

    def arrived(ref, j):
        return ref.at[j] if j < TICKS - 1 else ref.at[j, pl.ds(0, TENSOR - 1)]

    def merge(j):
        wait_bytes(arrived(stat_in, j), stat_recv.at[j])
        pages = stat_in[j].astype(f32)
        mixed = pages[:, 0:8, :]
        tops = pages[:, 8:9, :]
        totals = pages[:, 9:10, :] + pages[:, 10:11, :]
        top = jnp.max(tops, axis=0, keepdims=True)
        scale = jnp.exp(tops - top)
        total = jnp.sum(scale * totals, axis=0, keepdims=True)
        share = scale / total
        column = jnp.sum(jnp.where(mine[None], share, 0.0), axis=2, keepdims=True)
        mean = jnp.sum(column * mixed, axis=0)
        return mean, (top + jnp.log(total))[0]

    def combine(j, rows, merged):
        mean, level = merged
        wait_bytes(arrived(part_in, j), part_recv.at[j])
        sums = jnp.sum(part_in[j], axis=0)
        mean_sq = sums[3:4] / D + EPSILON
        own = sums[2:3] * lax.rsqrt(mean_sq * HD)
        share = 1.0 / (1.0 + jnp.exp(level - own))
        inverse = lax.rsqrt(mean_sq)
        share_col = jnp.sum(jnp.where(mine, share, 0.0), axis=1, keepdims=True)
        inverse_col = jnp.sum(jnp.where(mine, inverse, 0.0), axis=1, keepdims=True)
        fresh = jnp.where(even_row, sums[0:1], sums[1:2]) * inverse_col
        return (rows + (mean + share_col * (fresh - mean))).astype(bf16).astype(f32)

    def project(j, rows, turned=None):
        scaled = features_of(rows * gain8).astype(bf16)
        if turned is None:
            own_part = jnp.dot(scaled, folded[j], preferred_element_type=f32)
        else:
            key_part = jnp.dot(scaled, kw[...], preferred_element_type=f32).astype(bf16)
            own_part = jnp.dot(key_part, turned, preferred_element_type=f32)
        load_wait("vw", j == 0)
        value_part = jnp.dot(scaled, vw[...], preferred_element_type=f32)
        own_row = jnp.where(even_lane, own_part[0:1], own_part[1:2])
        square = rows * rows
        square = square[0:2] + square[2:4] + square[4:6] + square[6:8]
        square = jnp.sum(square, axis=1, keepdims=True)
        square_row = jnp.where(even_lane, square[0:1], square[1:2])
        tail = jnp.concatenate([own_row, square_row], axis=0)
        for k in range(KVH):
            part_out[j, k] = jnp.concatenate(
                [value_part[:, HD * k : HD * k + HD], tail], axis=0
            )

    def load_wait(name, wanted=True):
        if wanted:
            load[name].wait()

    def send_parts(j):
        send_page(lambda to: part_out.at[j, to // 4], part_in, j, part_send, part_recv)
        if j == TICKS - 1:
            part_in[j, ten] = part_out[j, ten // 4]

    def row_copy(j):
        return pltpu.make_async_remote_copy(
            row_out.at[j],
            row_in.at[j],
            row_send.at[j],
            row_recv.at[j],
            device_id=(following, ten),
            device_id_type=MESH,
        )

    def send_rows(j):
        @pl.when(jnp.logical_not(last))
        def _():
            row_copy(j).start()

    load["q"].wait()
    columns, turned = query_columns(0)
    load["hidden"].wait()
    load["gain"].wait()
    gain8 = heads_of(jnp.broadcast_to(gain_ref[...].astype(f32), (2, 512)))
    rows = heads_of(hidden_ref[...].astype(f32))
    row_out[0] = rows
    load["kw"].wait()
    project(0, rows, turned)
    load["ck"].wait()
    load["cv"].wait()
    stats(0, columns)
    load["entering"].wait()

    @pl.when(first)
    def _():
        pl.semaphore_wait(barrier, 2 * TENSOR - 1)

    @pl.when(jnp.logical_not(jnp.logical_or(first, last)))
    def _():
        pl.semaphore_wait(barrier, TENSOR)

    send_parts(0)
    send_stats(0)
    send_rows(0)
    columns, turned = query_columns(1)
    fold(1, turned)
    stats(1, columns)
    send_stats(1)
    for j in range(1, TICKS):

        @pl.when(first)
        def _():
            row_out[j] = heads_of(entering_ref[j - 1].astype(f32))

        @pl.when(jnp.logical_not(first))
        def _():
            row_copy(j - 1).wait_recv()
            merged = merge(j - 1)
            row_out[j] = combine(j - 1, row_in[j - 1], merged)

        rows = row_out[j]
        project(j, rows)
        send_parts(j)
        if j < TICKS - 1:
            send_rows(j)
            columns, turned = query_columns(j + 1)
            fold(j + 1, turned)
            stats(j + 1, columns)
            send_stats(j + 1)
    merged = merge(TICKS - 1)
    final = combine(TICKS - 1, rows, merged)
    out_ref[0] = features_of(final).astype(bf16)

    @pl.when(jnp.logical_not(last))
    def _():
        for j in range(TICKS - 1):
            wait_bytes(part_in.at[j], part_send.at[j])
            wait_bytes(stat_in.at[j], stat_send.at[j])
            row_copy(j).wait_send()

    wait_bytes(arrived(part_in, TICKS - 1), part_send.at[TICKS - 1])
    wait_bytes(arrived(stat_in, TICKS - 1), stat_send.at[TICKS - 1])


def on_device(
    hidden_rows,
    entering_rows,
    norm_gain,
    key_weight,
    value_weight,
    queries,
    cache_keys,
    cache_values,
    lengths,
    plan,
):
    vmem = pl.BlockSpec(memory_space=pltpu.VMEM)
    anywhere = pl.BlockSpec(memory_space=pl.ANY)
    dma = pltpu.SemaphoreType.DMA
    return pl.pallas_call(
        kernel,
        out_shape=jax.ShapeDtypeStruct((1, 2, 512), bf16),
        in_specs=[anywhere] * 10,
        out_specs=vmem,
        scratch_shapes=[
            pltpu.SMEM((2, 4), jnp.int32),
            pltpu.SMEM((4,), jnp.int32),
            pltpu.VMEM((2, 512), bf16),
            pltpu.VMEM((3, 2, 512), bf16),
            pltpu.VMEM((1, 512), bf16),
            pltpu.VMEM((512, 512), bf16),
            pltpu.VMEM((512, 512), bf16),
            pltpu.VMEM((4, 2, 8192), bf16),
            pltpu.VMEM((4, 2, 128, 512), bf16),
            pltpu.VMEM((4, 2, 128, 512), bf16),
            pltpu.VMEM((128, 128), f32),
            pltpu.VMEM((TICKS, 512, 128), bf16),
            pltpu.VMEM((TICKS, KVH, 4, 128), f32),
            pltpu.VMEM((TICKS, TENSOR, 4, 128), f32),
            pltpu.VMEM((TICKS, TENSOR, 16, 128), bf16),
            pltpu.VMEM((TICKS, TENSOR, 16, 128), bf16),
            pltpu.VMEM((TICKS, 8, 128), f32),
            pltpu.VMEM((TICKS - 1, 8, 128), f32),
            dma((10,)),
            dma((TICKS,)),
            dma((TICKS,)),
            dma((TICKS,)),
            dma((TICKS,)),
            dma((TICKS - 1,)),
            dma((TICKS - 1,)),
        ],
        compiler_params=pltpu.CompilerParams(
            collective_id=0, has_side_effects=True, vmem_limit_bytes=60 * 1024 * 1024
        ),
    )(
        hidden_rows,
        entering_rows,
        norm_gain,
        key_weight,
        value_weight,
        queries,
        cache_keys,
        cache_values,
        lengths.T,
        plan,
    )


def solution(mesh):
    in_specs = (
        P("section", None, "tensor"),
        P(None, None, "tensor"),
        P("section", "tensor"),
        P("section", "tensor", None),
        P("section", "tensor", None),
        P("section", None, None, None),
        P("section", None, None, "tensor", None),
        P("section", None, None, "tensor", None),
        P(),
        P(),
    )
    out_specs = P("section", None, "tensor")
    return jax.shard_map(
        on_device, mesh=mesh, in_specs=in_specs, out_specs=out_specs, check_vma=False
    )
```

```python
import functools

import jax
import jax.numpy as jnp
from jax import lax
from jax.experimental import pallas as pl
from jax.experimental.pallas import tpu as pltpu
from jax.sharding import PartitionSpec as P

D = 8192
HQ = 64
KVH = 4
HD = 128
TICKS = 4
TENSOR = 16
EPSILON = 1e-05
NEG_BIG = -1e30
MESH = pl.DeviceIdType.MESH
f32 = jnp.float32
bf16 = jnp.bfloat16


def iota(shape, axis):
    return lax.broadcasted_iota(jnp.int32, shape, axis)


def block_diagonal(columns):
    group = iota((HD, HD), 1) // 32
    return jnp.concatenate(
        [jnp.where(group == k, columns, 0.0) for k in range(KVH)], axis=0
    ).astype(bf16)


def kernel(
    hidden_hbm,
    entering_hbm,
    gain_hbm,
    kw_hbm,
    vw_hbm,
    q_hbm,
    ck_hbm,
    cv_hbm,
    len_hbm,
    plan_hbm,
    out_ref,
    len_ref,
    plan_ref,
    hidden_ref,
    entering_ref,
    gain_ref,
    kw,
    vw,
    qv,
    ck,
    cv,
    qs,
    folded,
    part_out,
    part_in,
    stat_out,
    stat_in,
    mixed_in,
    row_out,
    row_in,
    load_sem,
    part_send,
    part_recv,
    stat_send,
    stat_recv,
    row_send,
    row_recv,
):
    sections = lax.axis_size("section")
    sec = lax.axis_index("section")
    ten = lax.axis_index("tensor")
    following = lax.rem(sec + 1, sections)
    previous = lax.rem(sec + sections - 1, sections)

    first = sec == 0
    last = sec == sections - 1
    chip = ten // 2 * 2
    partner = chip + 1 - lax.rem(ten, 2)
    others = [lax.rem(chip + m, TENSOR) for m in (8, 9, 6, 7, 10, 11, 4, 5, 12, 13, 2, 3, 14, 15)]

    barrier = pltpu.get_barrier_semaphore()

    @pl.when(jnp.logical_not(first))
    def _():
        for k in others + [partner, ten]:
            pl.semaphore_signal(barrier, inc=1, device_id=(previous, k), device_id_type=MESH)

    @pl.when(first)
    def _():
        for k in others + [partner]:
            pl.semaphore_signal(barrier, inc=1, device_id=(sec, k), device_id_type=MESH)

    load = {}
    for i, (name, src, dst) in enumerate(
        [
            ("plan", plan_hbm, plan_ref),
            ("len", len_hbm, len_ref),
            ("q", q_hbm.at[0], qv),
            ("hidden", hidden_hbm.at[0], hidden_ref),
            ("gain", gain_hbm, gain_ref),
            ("kw", kw_hbm.at[0], kw),
            ("ck", ck_hbm.at[0], ck),
            ("vw", vw_hbm.at[0], vw),
            ("cv", cv_hbm.at[0], cv),
            ("entering", entering_hbm, entering_ref),
        ]
    ):
        load[name] = pltpu.make_async_copy(src, dst, load_sem.at[i])
        load[name].start()

    load["plan"].wait()
    load["len"].wait()
    slots = [plan_ref[lax.rem(sec + TICKS - j, TICKS)] for j in range(TICKS)]
    spans = [[len_ref[r, slots[j]] for r in range(2)] for j in range(TICKS)]

    row8 = iota((8, HD), 0)
    lane8 = iota((8, HD), 1)
    even_row = row8 % 2 == 0
    lane1 = iota((1, HD), 1)
    even_lane = lane1 % 2 == 0
    mine = lane8 == row8 + ten * 8
    mine_square = lane8 == lax.rem(row8 + ten * 8 + 64, HD)

    def heads_of(block):
        return jnp.concatenate([block[:, h * HD : (h + 1) * HD] for h in range(4)], axis=0)

    def features_of(block):
        return jnp.concatenate([block[2 * h : 2 * h + 2, :] for h in range(4)], axis=1)

    angle_rows = jnp.zeros((8, HD), f32)
    for j in range(TICKS):
        for r in range(2):
            angle_rows = jnp.where(row8 == 2 * j + r, spans[j][r].astype(f32), angle_rows)
    rates = jnp.exp((lane8 % 64).astype(f32) * (-2.0 * jnp.log(f32(500000.0)) / HD))
    angle = angle_rows * rates
    cosines = jnp.cos(angle)
    sines = jnp.sin(angle)
    sines = jnp.where(lane8 < 64, sines, -sines)

    def query_columns(j):
        rows = qv[slots[j]].astype(f32)
        for h in range(HQ):
            qs[2 * h : 2 * h + 2, :] = rows[:, h * HD : (h + 1) * HD]
        q = qs[...]
        cos8 = jnp.concatenate([cosines[2 * j : 2 * j + 2]] * 4, axis=0)
        sin8 = jnp.concatenate([sines[2 * j : 2 * j + 2]] * 4, axis=0)
        other = pltpu.roll(q, 64, 1)
        turned = (
            q.reshape(16, 8, HD) * cos8[None] + other.reshape(16, 8, HD) * sin8[None]
        ).reshape(HD, HD)
        return block_diagonal(q.T), block_diagonal(turned.T)

    def fold(j, turned):
        folded[j] = jnp.dot(kw[...], turned, preferred_element_type=f32).astype(bf16)

    def stats(j, columns):
        keys = ck[slots[j]].reshape(256, 512)
        both = jnp.dot(keys, columns, preferred_element_type=f32)
        scores = jnp.where(even_lane, both[:HD], both[HD:]) * HD ** (-0.5)
        span = jnp.where(even_lane, spans[j][0], spans[j][1])
        valid = iota((HD, HD), 0) + ten * HD < span
        scores = jnp.where(valid, scores, NEG_BIG)
        top = jnp.max(scores, axis=0, keepdims=True).astype(bf16).astype(f32)
        weights = jnp.where(valid, jnp.exp(scores - top), 0.0).astype(bf16).astype(f32)
        total = jnp.sum(weights, axis=0, keepdims=True)
        turned = weights.T
        even = iota((HD, HD), 0) % 2 == 0
        wide = jnp.concatenate(
            [jnp.where(even, turned, 0.0), jnp.where(even, 0.0, turned)], axis=1
        ).astype(bf16)
        values = cv[slots[j]].reshape(256, 512)
        level = jnp.concatenate([top, total], axis=0).astype(bf16)
        for k in range(KVH):
            mixed = jnp.dot(
                wide[32 * k : 32 * k + 32],
                values[:, HD * k : HD * k + HD],
                preferred_element_type=f32,
            )
            for i in range(4):
                for p in range(4):
                    at = 8 * i + 2 * p
                    stat_out[j, 4 * k + i, p] = mixed[at : at + 2].astype(bf16)
                stat_out[j, 4 * k + i, 4] = level

    def send_page(source, target, j, send, receive):
        def to_section(section, partners):
            for to in partners:
                pltpu.make_async_remote_copy(
                    source(to),
                    target.at[j, ten],
                    send.at[j],
                    receive.at[j],
                    device_id=(section, to),
                    device_id_type=MESH,
                ).start()

        if j < TICKS - 1:

            @pl.when(jnp.logical_not(last))
            def _():
                to_section(following, others + [partner, ten])
        else:
            to_section(sec, others + [partner])

    def send_stats(j):
        send_page(lambda to: stat_out.at[j, to], stat_in, j, stat_send, stat_recv)
        if j == TICKS - 1:
            stat_in[j, ten] = stat_out[j, ten]

    def wait_bytes(ref, sem):
        pltpu.make_async_copy(ref, ref, sem).wait()

    def arrived(ref, j):
        return ref.at[j] if j < TICKS - 1 else ref.at[j, pl.ds(0, TENSOR - 1)]

    def merge(j):
        wait_bytes(arrived(stat_in, j), stat_recv.at[j])
        for k in range(TENSOR):
            for p in range(4):
                mixed_in[k, 2 * p : 2 * p + 2] = stat_in[j, k, p].astype(f32)
        mixed = mixed_in[...]
        levels = stat_in[j, :, 4].astype(f32)
        tops = levels[:, 0:1, :]
        totals = levels[:, 1:2, :]
        top = jnp.max(tops, axis=0, keepdims=True)
        scale = jnp.exp(tops - top)
        total = jnp.sum(scale * totals, axis=0, keepdims=True)
        share = scale / total
        column = jnp.sum(jnp.where(mine[None], share, 0.0), axis=2, keepdims=True)
        mean = jnp.sum(column * mixed, axis=0)
        level = (top + jnp.log(total))[0]
        return mean, jnp.sum(jnp.where(mine, level, 0.0), axis=1, keepdims=True)

    def combine(j, rows, merged):
        mean, level = merged
        wait_bytes(arrived(part_in, j), part_recv.at[j])
        sums = jnp.sum(part_in[j].astype(f32), axis=0)
        mixture = sums[2:3] + sums[3:4]
        own_col = jnp.sum(jnp.where(mine, mixture, 0.0), axis=1, keepdims=True)
        square_col = jnp.sum(jnp.where(mine_square, mixture, 0.0), axis=1, keepdims=True)
        inverse = lax.rsqrt(square_col / D + EPSILON)
        share = 1.0 / (1.0 + jnp.exp(level - own_col * inverse * HD ** (-0.5)))
        fresh = jnp.where(even_row, sums[0:1], sums[1:2]) * inverse
        return (rows + (mean + share * (fresh - mean))).astype(bf16).astype(f32)

    def project(j, rows, turned=None):
        scaled = features_of(rows * gain8).astype(bf16)
        if turned is None:
            own_part = jnp.dot(scaled, folded[j], preferred_element_type=f32)
        else:
            key_part = jnp.dot(scaled, kw[...], preferred_element_type=f32).astype(bf16)
            own_part = jnp.dot(key_part, turned, preferred_element_type=f32)
        load_wait("vw", j == 0)
        value_part = jnp.dot(scaled, vw[...], preferred_element_type=f32)
        own_row = jnp.where(even_lane, own_part[0:1], own_part[1:2])
        square = rows * rows
        square = square[0:2] + square[2:4] + square[4:6] + square[6:8]
        square = jnp.sum(square, axis=1, keepdims=True)
        square_row = jnp.where(even_lane, square[0:1], square[1:2])
        for k in range(KVH):
            mixture = jnp.where(lane1 // 32 == k, own_row, square_row)
            high = mixture.astype(bf16).astype(f32)
            part_out[j, k] = jnp.concatenate(
                [value_part[:, HD * k : HD * k + HD], high, mixture - high], axis=0
            ).astype(bf16)

    def load_wait(name, wanted=True):
        if wanted:
            load[name].wait()

    def send_parts(j):
        send_page(lambda to: part_out.at[j, to // 4], part_in, j, part_send, part_recv)
        if j == TICKS - 1:
            part_in[j, ten] = part_out[j, ten // 4]

    def row_copy(j):
        return pltpu.make_async_remote_copy(
            row_out.at[j],
            row_in.at[j],
            row_send.at[j],
            row_recv.at[j],
            device_id=(following, ten),
            device_id_type=MESH,
        )

    def send_rows(j):
        @pl.when(jnp.logical_not(last))
        def _():
            row_copy(j).start()

    load["q"].wait()
    columns, turned = query_columns(0)
    load["hidden"].wait()
    load["gain"].wait()
    gain8 = heads_of(jnp.broadcast_to(gain_ref[...].astype(f32), (2, 512)))
    rows = heads_of(hidden_ref[...].astype(f32))
    row_out[0] = rows
    load["kw"].wait()
    project(0, rows, turned)
    load["ck"].wait()
    load["cv"].wait()
    stats(0, columns)
    load["entering"].wait()

    @pl.when(first)
    def _():
        pl.semaphore_wait(barrier, 2 * TENSOR - 1)

    @pl.when(jnp.logical_not(jnp.logical_or(first, last)))
    def _():
        pl.semaphore_wait(barrier, TENSOR)

    send_parts(0)
    send_stats(0)
    send_rows(0)
    columns, turned = query_columns(1)
    fold(1, turned)
    stats(1, columns)
    send_stats(1)
    for j in range(1, TICKS):

        @pl.when(first)
        def _():
            row_out[j] = heads_of(entering_ref[j - 1].astype(f32))

        @pl.when(jnp.logical_not(first))
        def _():
            row_copy(j - 1).wait_recv()
            merged = merge(j - 1)
            row_out[j] = combine(j - 1, row_in[j - 1], merged)

        rows = row_out[j]
        project(j, rows)
        send_parts(j)
        if j < TICKS - 1:
            send_rows(j)
            columns, turned = query_columns(j + 1)
            fold(j + 1, turned)
            stats(j + 1, columns)
            send_stats(j + 1)
    merged = merge(TICKS - 1)
    final = combine(TICKS - 1, rows, merged)
    out_ref[0] = features_of(final).astype(bf16)

    @pl.when(jnp.logical_not(last))
    def _():
        for j in range(TICKS - 1):
            wait_bytes(part_in.at[j], part_send.at[j])
            wait_bytes(stat_in.at[j], stat_send.at[j])
            row_copy(j).wait_send()

    wait_bytes(arrived(part_in, TICKS - 1), part_send.at[TICKS - 1])
    wait_bytes(arrived(stat_in, TICKS - 1), stat_send.at[TICKS - 1])


def on_device(
    hidden_rows,
    entering_rows,
    norm_gain,
    key_weight,
    value_weight,
    queries,
    cache_keys,
    cache_values,
    lengths,
    plan,
):
    vmem = pl.BlockSpec(memory_space=pltpu.VMEM)
    anywhere = pl.BlockSpec(memory_space=pl.ANY)
    dma = pltpu.SemaphoreType.DMA
    return pl.pallas_call(
        kernel,
        out_shape=pltpu.VMEM((1, 2, 512), bf16),
        in_specs=[anywhere] * 10,
        out_specs=vmem,
        scratch_shapes=[
            pltpu.SMEM((2, 4), jnp.int32),
            pltpu.SMEM((4,), jnp.int32),
            pltpu.VMEM((2, 512), bf16),
            pltpu.VMEM((3, 2, 512), bf16),
            pltpu.VMEM((1, 512), bf16),
            pltpu.VMEM((512, 512), bf16),
            pltpu.VMEM((512, 512), bf16),
            pltpu.VMEM((4, 2, 8192), bf16),
            pltpu.VMEM((4, 2, 128, 512), bf16),
            pltpu.VMEM((4, 2, 128, 512), bf16),
            pltpu.VMEM((128, 128), f32),
            pltpu.VMEM((TICKS, 512, 128), bf16),
            pltpu.VMEM((TICKS, KVH, 4, 128), bf16),
            pltpu.VMEM((TICKS, TENSOR, 4, 128), bf16),
            pltpu.VMEM((TICKS, TENSOR, 5, 2, 128), bf16),
            pltpu.VMEM((TICKS, TENSOR, 5, 2, 128), bf16),
            pltpu.VMEM((TENSOR, 8, 128), f32),
            pltpu.VMEM((TICKS, 8, 128), f32),
            pltpu.VMEM((TICKS - 1, 8, 128), f32),
            dma((10,)),
            dma((TICKS,)),
            dma((TICKS,)),
            dma((TICKS,)),
            dma((TICKS,)),
            dma((TICKS - 1,)),
            dma((TICKS - 1,)),
        ],
        compiler_params=pltpu.CompilerParams(
            collective_id=0, has_side_effects=True, vmem_limit_bytes=60 * 1024 * 1024
        ),
    )(
        hidden_rows,
        entering_rows,
        norm_gain,
        key_weight,
        value_weight,
        queries,
        cache_keys,
        cache_values,
        lengths.T,
        plan,
    )


def solution(mesh):
    in_specs = (
        P("section", None, "tensor"),
        P(None, None, "tensor"),
        P("section", "tensor"),
        P("section", "tensor", None),
        P("section", "tensor", None),
        P("section", None, None, None),
        P("section", None, None, "tensor", None),
        P("section", None, None, "tensor", None),
        P(),
        P(),
    )
    out_specs = P("section", None, "tensor")
    return jax.shard_map(
        on_device, mesh=mesh, in_specs=in_specs, out_specs=out_specs, check_vma=False
    )
```

```python
import functools

import jax
import jax.numpy as jnp
from jax import lax
from jax.experimental import pallas as pl
from jax.experimental.pallas import tpu as pltpu
from jax.sharding import PartitionSpec as P

D = 8192
HQ = 64
KVH = 4
HD = 128
TICKS = 4
TENSOR = 16
EPSILON = 1e-05
NEG_BIG = -1e30
MESH = pl.DeviceIdType.MESH
f32 = jnp.float32
bf16 = jnp.bfloat16


def iota(shape, axis):
    return lax.broadcasted_iota(jnp.int32, shape, axis)


def block_diagonal(columns):
    group = iota((HD, HD), 1) // 32
    return jnp.concatenate(
        [jnp.where(group == k, columns, 0.0) for k in range(KVH)], axis=0
    ).astype(bf16)


def kernel(
    hidden_hbm,
    entering_hbm,
    gain_hbm,
    kw_hbm,
    vw_hbm,
    q_hbm,
    ck_hbm,
    cv_hbm,
    len_hbm,
    plan_hbm,
    out_ref,
    len_ref,
    plan_ref,
    hidden_ref,
    entering_ref,
    gain_ref,
    kw,
    vw,
    qv,
    ck,
    cv,
    qs,
    folded,
    part_out,
    part_in,
    stat_out,
    stat_in,
    mixed_in,
    row_out,
    row_in,
    load_sem,
    part_send,
    part_recv,
    stat_send,
    stat_recv,
    row_send,
    row_recv,
):
    sections = lax.axis_size("section")
    sec = lax.axis_index("section")
    ten = lax.axis_index("tensor")
    following = lax.rem(sec + 1, sections)
    previous = lax.rem(sec + sections - 1, sections)

    first = sec == 0
    last = sec == sections - 1
    chip = ten // 2 * 2
    partner = chip + 1 - lax.rem(ten, 2)
    others = [lax.rem(chip + m, TENSOR) for m in (8, 9, 6, 7, 10, 11, 4, 5, 12, 13, 2, 3, 14, 15)]

    barrier = pltpu.get_barrier_semaphore()

    @pl.when(jnp.logical_not(first))
    def _():
        for k in others + [partner, ten]:
            pl.semaphore_signal(barrier, inc=1, device_id=(previous, k), device_id_type=MESH)

    @pl.when(first)
    def _():
        for k in others + [partner]:
            pl.semaphore_signal(barrier, inc=1, device_id=(sec, k), device_id_type=MESH)

    load = {}
    for i, (name, src, dst) in enumerate(
        [
            ("plan", plan_hbm, plan_ref),
            ("len", len_hbm, len_ref),
            ("q", q_hbm.at[0], qv),
            ("hidden", hidden_hbm.at[0], hidden_ref),
            ("gain", gain_hbm, gain_ref),
            ("kw", kw_hbm.at[0], kw),
            ("ck", ck_hbm.at[0], ck),
            ("vw", vw_hbm.at[0], vw),
            ("cv", cv_hbm.at[0], cv),
            ("entering", entering_hbm, entering_ref),
        ]
    ):
        load[name] = pltpu.make_async_copy(src, dst, load_sem.at[i])
        load[name].start()

    load["plan"].wait()
    load["len"].wait()
    slots = [plan_ref[lax.rem(sec + TICKS - j, TICKS)] for j in range(TICKS)]
    spans = [[len_ref[r, slots[j]] for r in range(2)] for j in range(TICKS)]

    row8 = iota((8, HD), 0)
    lane8 = iota((8, HD), 1)
    even_row = row8 % 2 == 0
    lane1 = iota((1, HD), 1)
    even_lane = lane1 % 2 == 0
    mine = lane8 == row8 + ten * 8
    mine_square = lane8 == lax.rem(row8 + ten * 8 + 64, HD)

    def heads_of(block):
        return jnp.concatenate([block[:, h * HD : (h + 1) * HD] for h in range(4)], axis=0)

    def features_of(block):
        return jnp.concatenate([block[2 * h : 2 * h + 2, :] for h in range(4)], axis=1)

    angle_rows = jnp.zeros((8, HD), f32)
    for j in range(TICKS):
        for r in range(2):
            angle_rows = jnp.where(row8 == 2 * j + r, spans[j][r].astype(f32), angle_rows)
    rates = jnp.exp((lane8 % 64).astype(f32) * (-2.0 * jnp.log(f32(500000.0)) / HD))
    angle = angle_rows * rates
    cosines = jnp.cos(angle)
    sines = jnp.sin(angle)
    sines = jnp.where(lane8 < 64, sines, -sines)

    def query_columns(j):
        rows = qv[slots[j]].astype(f32)
        for h in range(HQ):
            qs[2 * h : 2 * h + 2, :] = rows[:, h * HD : (h + 1) * HD]
        q = qs[...]
        cos8 = jnp.concatenate([cosines[2 * j : 2 * j + 2]] * 4, axis=0)
        sin8 = jnp.concatenate([sines[2 * j : 2 * j + 2]] * 4, axis=0)
        other = pltpu.roll(q, 64, 1)
        turned = (
            q.reshape(16, 8, HD) * cos8[None] + other.reshape(16, 8, HD) * sin8[None]
        ).reshape(HD, HD)
        return block_diagonal(q.T), block_diagonal(turned.T)

    def fold(j, turned):
        folded[j] = jnp.dot(kw[...], turned, preferred_element_type=f32).astype(bf16)

    def stats(j, columns):
        keys = ck[slots[j]].reshape(256, 512)
        both = jnp.dot(keys, columns, preferred_element_type=f32)
        scores = jnp.where(even_lane, both[:HD], both[HD:]) * HD ** (-0.5)
        span = jnp.where(even_lane, spans[j][0], spans[j][1])
        valid = iota((HD, HD), 0) + ten * HD < span
        scores = jnp.where(valid, scores, NEG_BIG)
        top = jnp.max(scores, axis=0, keepdims=True).astype(bf16).astype(f32)
        weights = jnp.where(valid, jnp.exp(scores - top), 0.0).astype(bf16).astype(f32)
        total = jnp.sum(weights, axis=0, keepdims=True)
        turned = weights.T
        even = iota((HD, HD), 0) % 2 == 0
        wide = jnp.concatenate(
            [jnp.where(even, turned, 0.0), jnp.where(even, 0.0, turned)], axis=1
        ).astype(bf16)
        values = cv[slots[j]].reshape(256, 512)
        level = jnp.concatenate([top, total], axis=0).astype(bf16)
        for k in range(KVH):
            mixed = jnp.dot(
                wide[32 * k : 32 * k + 32],
                values[:, HD * k : HD * k + HD],
                preferred_element_type=f32,
            )
            for i in range(4):
                for p in range(4):
                    at = 8 * i + 2 * p
                    stat_out[j, 4 * k + i, p] = mixed[at : at + 2].astype(bf16)
                stat_out[j, 4 * k + i, 4] = level

    def send_pages(j, kinds):
        def to_section(section, partners):
            for to in partners:
                for source, target, send, receive in kinds:
                    pltpu.make_async_remote_copy(
                        source(to),
                        target.at[j, ten],
                        send.at[j],
                        receive.at[j],
                        device_id=(section, to),
                        device_id_type=MESH,
                    ).start()

        if j < TICKS - 1:

            @pl.when(jnp.logical_not(last))
            def _():
                to_section(following, others + [partner, ten])
        else:
            to_section(sec, others + [partner])

    def stat_pages(j):
        return (lambda to: stat_out.at[j, to], stat_in, stat_send, stat_recv)

    def part_pages(j):
        return (lambda to: part_out.at[j, to // 4], part_in, part_send, part_recv)

    def send_stats(j):
        send_pages(j, [stat_pages(j)])
        if j == TICKS - 1:
            stat_in[j, ten] = stat_out[j, ten]

    def send_parts(j):
        send_pages(j, [part_pages(j)])
        if j == TICKS - 1:
            part_in[j, ten] = part_out[j, ten // 4]

    def wait_bytes(ref, sem):
        pltpu.make_async_copy(ref, ref, sem).wait()

    def arrived(ref, j):
        return ref.at[j] if j < TICKS - 1 else ref.at[j, pl.ds(0, TENSOR - 1)]

    def merge(j):
        wait_bytes(arrived(stat_in, j), stat_recv.at[j])
        for k in range(TENSOR):
            for p in range(4):
                mixed_in[k, 2 * p : 2 * p + 2] = stat_in[j, k, p].astype(f32)
        mixed = mixed_in[...]
        levels = stat_in[j, :, 4].astype(f32)
        tops = levels[:, 0:1, :]
        totals = levels[:, 1:2, :]
        top = jnp.max(tops, axis=0, keepdims=True)
        scale = jnp.exp(tops - top)
        total = jnp.sum(scale * totals, axis=0, keepdims=True)
        share = scale / total
        column = jnp.sum(jnp.where(mine[None], share, 0.0), axis=2, keepdims=True)
        mean = jnp.sum(column * mixed, axis=0)
        level = (top + jnp.log(total))[0]
        return mean, jnp.sum(jnp.where(mine, level, 0.0), axis=1, keepdims=True)

    def arrival(j, level):
        wait_bytes(arrived(part_in, j), part_recv.at[j])
        sums = jnp.sum(part_in[j].astype(f32), axis=0)
        mixture = sums[2:3] + sums[3:4]
        own_col = jnp.sum(jnp.where(mine, mixture, 0.0), axis=1, keepdims=True)
        square_col = jnp.sum(jnp.where(mine_square, mixture, 0.0), axis=1, keepdims=True)
        inverse = lax.rsqrt(square_col / D + EPSILON)
        share = 1.0 / (1.0 + jnp.exp(level - own_col * inverse * HD ** (-0.5)))
        return share, inverse, jnp.where(even_row, sums[0:1], sums[1:2])

    def project(j, rows, turned=None):
        scaled = features_of(rows * gain8).astype(bf16)
        if turned is None:
            own_part = jnp.dot(scaled, folded[j], preferred_element_type=f32)
        else:
            key_part = jnp.dot(scaled, kw[...], preferred_element_type=f32).astype(bf16)
            own_part = jnp.dot(key_part, turned, preferred_element_type=f32)
        load_wait("vw", j == 0)
        value_part = jnp.dot(scaled, vw[...], preferred_element_type=f32)
        square = rows * rows
        square = square[0:2] + square[2:4] + square[4:6] + square[6:8]
        square = jnp.sum(square, axis=1, keepdims=True)
        write_parts(j, value_part, own_part, square)

    def write_parts(j, values, own, square):
        own_row = jnp.where(even_lane, own[0:1], own[1:2])
        square_row = jnp.where(even_lane, square[0:1], square[1:2])
        for k in range(KVH):
            mixture = jnp.where(lane1 // 32 == k, own_row, square_row)
            high = mixture.astype(bf16).astype(f32)
            part_out[j, k] = jnp.concatenate(
                [values[0:2, HD * k : HD * k + HD], high, mixture - high], axis=0
            ).astype(bf16)

    def blocks(rows):
        return jnp.concatenate(
            [jnp.where(row8 // 2 == h, rows, 0.0) for h in range(4)], axis=1
        ).astype(bf16)

    def over_heads(rows):
        rows = rows + pltpu.roll(rows, 4, 0)
        return rows + pltpu.roll(rows, 2, 0)

    def dots(left, right):
        return jnp.sum(left * right, axis=1, keepdims=True)

    def advance(j):
        row_copy(j - 1).wait_recv()
        rows = row_in[j - 1]
        mean, level = merge(j - 1)
        known = jnp.concatenate([blocks(rows * gain8), blocks(mean * gain8)], axis=0)
        known_value = jnp.dot(known, vw[...], preferred_element_type=f32)
        known_own = jnp.dot(known, folded[j], preferred_element_type=f32)
        rows_rows, rows_mean, mean_mean = dots(rows, rows), dots(rows, mean), dots(mean, mean)
        share, inverse, fresh = arrival(j - 1, level)
        scaled = blocks(fresh * gain8)
        fresh_value = jnp.dot(scaled, vw[...], preferred_element_type=f32)
        fresh_own = jnp.dot(scaled, folded[j], preferred_element_type=f32)
        rest = 1.0 - share
        factor = share * inverse
        square = (
            rows_rows
            + rest * (2.0 * rows_mean + rest * mean_mean)
            + factor * (2.0 * (dots(rows, fresh) + rest * dots(mean, fresh)) + factor * dots(fresh, fresh))
        )
        write_parts(
            j,
            over_heads(known_value[:8] + rest * known_value[8:] + factor * fresh_value),
            over_heads(known_own[:8] + rest * known_own[8:] + factor * fresh_own),
            over_heads(jnp.broadcast_to(square, (8, HD))),
        )
        row_out[j] = (rows + rest * mean + factor * fresh).astype(bf16).astype(f32)

    def load_wait(name, wanted=True):
        if wanted:
            load[name].wait()

    def row_copy(j):
        return pltpu.make_async_remote_copy(
            row_out.at[j],
            row_in.at[j],
            row_send.at[j],
            row_recv.at[j],
            device_id=(following, ten),
            device_id_type=MESH,
        )

    def send_rows(j):
        @pl.when(jnp.logical_not(last))
        def _():
            row_copy(j).start()

    load["q"].wait()
    columns, turned = query_columns(0)
    load["hidden"].wait()
    load["gain"].wait()
    gain8 = heads_of(jnp.broadcast_to(gain_ref[...].astype(f32), (2, 512)))
    rows = heads_of(hidden_ref[...].astype(f32))
    row_out[0] = rows
    load["kw"].wait()
    project(0, rows, turned)
    load["ck"].wait()
    load["cv"].wait()
    stats(0, columns)
    load["entering"].wait()

    @pl.when(first)
    def _():
        pl.semaphore_wait(barrier, 2 * TENSOR - 1)

    @pl.when(jnp.logical_not(jnp.logical_or(first, last)))
    def _():
        pl.semaphore_wait(barrier, TENSOR)

    send_pages(0, [part_pages(0), stat_pages(0)])
    send_rows(0)
    columns, turned = query_columns(1)
    fold(1, turned)
    stats(1, columns)
    send_stats(1)
    for j in range(1, TICKS):

        @pl.when(first)
        def _():
            rows = heads_of(entering_ref[j - 1].astype(f32))
            row_out[j] = rows
            project(j, rows)

        @pl.when(jnp.logical_not(first))
        def _():
            advance(j)

        send_parts(j)
        if j < TICKS - 1:
            send_rows(j)
            columns, turned = query_columns(j + 1)
            fold(j + 1, turned)
            stats(j + 1, columns)
            send_stats(j + 1)
    rows = row_out[TICKS - 1]
    mean, level = merge(TICKS - 1)
    share, inverse, fresh = arrival(TICKS - 1, level)
    final = rows + (mean + share * (fresh * inverse - mean))
    out_ref[0] = features_of(final).astype(bf16)

    @pl.when(jnp.logical_not(last))
    def _():
        for j in range(TICKS - 1):
            wait_bytes(part_in.at[j], part_send.at[j])
            wait_bytes(stat_in.at[j], stat_send.at[j])
            row_copy(j).wait_send()

    wait_bytes(arrived(part_in, TICKS - 1), part_send.at[TICKS - 1])
    wait_bytes(arrived(stat_in, TICKS - 1), stat_send.at[TICKS - 1])


def on_device(
    hidden_rows,
    entering_rows,
    norm_gain,
    key_weight,
    value_weight,
    queries,
    cache_keys,
    cache_values,
    lengths,
    plan,
):
    vmem = pl.BlockSpec(memory_space=pltpu.VMEM)
    anywhere = pl.BlockSpec(memory_space=pl.ANY)
    dma = pltpu.SemaphoreType.DMA
    return pl.pallas_call(
        kernel,
        out_shape=pltpu.VMEM((1, 2, 512), bf16),
        in_specs=[anywhere] * 10,
        out_specs=vmem,
        scratch_shapes=[
            pltpu.SMEM((2, 4), jnp.int32),
            pltpu.SMEM((4,), jnp.int32),
            pltpu.VMEM((2, 512), bf16),
            pltpu.VMEM((3, 2, 512), bf16),
            pltpu.VMEM((1, 512), bf16),
            pltpu.VMEM((512, 512), bf16),
            pltpu.VMEM((512, 512), bf16),
            pltpu.VMEM((4, 2, 8192), bf16),
            pltpu.VMEM((4, 2, 128, 512), bf16),
            pltpu.VMEM((4, 2, 128, 512), bf16),
            pltpu.VMEM((128, 128), f32),
            pltpu.VMEM((TICKS, 512, 128), bf16),
            pltpu.VMEM((TICKS, KVH, 4, 128), bf16),
            pltpu.VMEM((TICKS, TENSOR, 4, 128), bf16),
            pltpu.VMEM((TICKS, TENSOR, 5, 2, 128), bf16),
            pltpu.VMEM((TICKS, TENSOR, 5, 2, 128), bf16),
            pltpu.VMEM((TENSOR, 8, 128), f32),
            pltpu.VMEM((TICKS, 8, 128), f32),
            pltpu.VMEM((TICKS - 1, 8, 128), f32),
            dma((10,)),
            dma((TICKS,)),
            dma((TICKS,)),
            dma((TICKS,)),
            dma((TICKS,)),
            dma((TICKS - 1,)),
            dma((TICKS - 1,)),
        ],
        compiler_params=pltpu.CompilerParams(
            collective_id=0, has_side_effects=True, vmem_limit_bytes=60 * 1024 * 1024
        ),
    )(
        hidden_rows,
        entering_rows,
        norm_gain,
        key_weight,
        value_weight,
        queries,
        cache_keys,
        cache_values,
        lengths.T,
        plan,
    )


def solution(mesh):
    in_specs = (
        P("section", None, "tensor"),
        P(None, None, "tensor"),
        P("section", "tensor"),
        P("section", "tensor", None),
        P("section", "tensor", None),
        P("section", None, None, None),
        P("section", None, None, "tensor", None),
        P("section", None, None, "tensor", None),
        P(),
        P(),
    )
    out_specs = P("section", None, "tensor")
    return jax.shard_map(
        on_device, mesh=mesh, in_specs=in_specs, out_specs=out_specs, check_vma=False
    )
```

```python
import functools

import jax
import jax.numpy as jnp
from jax import lax
from jax.experimental import pallas as pl
from jax.experimental.pallas import tpu as pltpu
from jax.sharding import PartitionSpec as P

D = 8192
HQ = 64
KVH = 4
HD = 128
TICKS = 4
TENSOR = 16
EPSILON = 1e-05
SLOW_STEP = 15
ALONE = TICKS
NEG_BIG = -1e30
MESH = pl.DeviceIdType.MESH
f32 = jnp.float32
bf16 = jnp.bfloat16


def iota(shape, axis):
    return lax.broadcasted_iota(jnp.int32, shape, axis)


def block_diagonal(columns):
    group = iota((HD, HD), 1) // 32
    return jnp.concatenate(
        [jnp.where(group == k, columns, 0.0) for k in range(KVH)], axis=0
    ).astype(bf16)


def kernel(
    hidden_hbm,
    entering_hbm,
    gain_hbm,
    kw_hbm,
    vw_hbm,
    q_hbm,
    ck_hbm,
    cv_hbm,
    len_hbm,
    plan_hbm,
    out_ref,
    len_ref,
    plan_ref,
    hidden_ref,
    entering_ref,
    gain_ref,
    kw,
    vw,
    qv,
    ck,
    cv,
    qs,
    folded,
    part_out,
    part_in,
    stat_out,
    stat_in,
    mixed_in,
    row_out,
    row_in,
    load_sem,
    part_send,
    part_recv,
    stat_send,
    stat_recv,
    row_send,
    row_recv,
):
    sections = lax.axis_size("section")
    sec = lax.axis_index("section")
    ten = lax.axis_index("tensor")
    following = lax.rem(sec + 1, sections)
    previous = lax.rem(sec + sections - 1, sections)

    first = sec == 0
    last = sec == sections - 1
    alone = sec == SLOW_STEP
    after = sec == SLOW_STEP + 1
    chip = ten // 2 * 2
    partner = chip + 1 - lax.rem(ten, 2)
    others = [lax.rem(chip + m, TENSOR) for m in (8, 9, 6, 7, 10, 11, 4, 5, 12, 13, 2, 3, 14, 15)]

    barrier = pltpu.get_barrier_semaphore()

    @pl.when(jnp.logical_not(jnp.logical_or(first, after)))
    def _():
        for k in others + [partner, ten]:
            pl.semaphore_signal(barrier, inc=1, device_id=(previous, k), device_id_type=MESH)

    @pl.when(after)
    def _():
        pl.semaphore_signal(barrier, inc=1, device_id=(previous, ten), device_id_type=MESH)

    @pl.when(jnp.logical_or(first, alone))
    def _():
        for k in others + [partner]:
            pl.semaphore_signal(barrier, inc=1, device_id=(sec, k), device_id_type=MESH)

    load = {}
    for i, (name, src, dst) in enumerate(
        [
            ("plan", plan_hbm, plan_ref),
            ("len", len_hbm, len_ref),
            ("q", q_hbm.at[0], qv),
            ("hidden", hidden_hbm.at[0], hidden_ref),
            ("gain", gain_hbm, gain_ref),
            ("kw", kw_hbm.at[0], kw),
            ("ck", ck_hbm.at[0], ck),
            ("vw", vw_hbm.at[0], vw),
            ("cv", cv_hbm.at[0], cv),
            ("entering", entering_hbm, entering_ref),
        ]
    ):
        load[name] = pltpu.make_async_copy(src, dst, load_sem.at[i])
        load[name].start()

    load["plan"].wait()
    load["len"].wait()
    slots = [plan_ref[lax.rem(sec + TICKS - j, TICKS)] for j in range(TICKS)]
    spans = [[len_ref[r, slots[j]] for r in range(2)] for j in range(TICKS)]

    row8 = iota((8, HD), 0)
    lane8 = iota((8, HD), 1)
    even_row = row8 % 2 == 0
    lane1 = iota((1, HD), 1)
    even_lane = lane1 % 2 == 0
    mine = lane8 == row8 + ten * 8
    mine_square = lane8 == lax.rem(row8 + ten * 8 + 64, HD)

    def heads_of(block):
        return jnp.concatenate([block[:, h * HD : (h + 1) * HD] for h in range(4)], axis=0)

    def features_of(block):
        return jnp.concatenate([block[2 * h : 2 * h + 2, :] for h in range(4)], axis=1)

    angle_rows = jnp.zeros((8, HD), f32)
    for j in range(TICKS):
        for r in range(2):
            angle_rows = jnp.where(row8 == 2 * j + r, spans[j][r].astype(f32), angle_rows)
    rates = jnp.exp((lane8 % 64).astype(f32) * (-2.0 * jnp.log(f32(500000.0)) / HD))
    angle = angle_rows * rates
    cosines = jnp.cos(angle)
    sines = jnp.sin(angle)
    sines = jnp.where(lane8 < 64, sines, -sines)

    def query_columns(j):
        rows = qv[slots[j]].astype(f32)
        for h in range(HQ):
            qs[2 * h : 2 * h + 2, :] = rows[:, h * HD : (h + 1) * HD]
        q = qs[...]
        cos8 = jnp.concatenate([cosines[2 * j : 2 * j + 2]] * 4, axis=0)
        sin8 = jnp.concatenate([sines[2 * j : 2 * j + 2]] * 4, axis=0)
        other = pltpu.roll(q, 64, 1)
        turned = (
            q.reshape(16, 8, HD) * cos8[None] + other.reshape(16, 8, HD) * sin8[None]
        ).reshape(HD, HD)
        return block_diagonal(q.T), block_diagonal(turned.T)

    def fold(j, turned):
        folded[j] = jnp.dot(kw[...], turned, preferred_element_type=f32).astype(bf16)

    def stats(j, columns):
        keys = ck[slots[j]].reshape(256, 512)
        both = jnp.dot(keys, columns, preferred_element_type=f32)
        scores = jnp.where(even_lane, both[:HD], both[HD:]) * HD ** (-0.5)
        span = jnp.where(even_lane, spans[j][0], spans[j][1])
        valid = iota((HD, HD), 0) + ten * HD < span
        scores = jnp.where(valid, scores, NEG_BIG)
        top = jnp.max(scores, axis=0, keepdims=True).astype(bf16).astype(f32)
        weights = jnp.where(valid, jnp.exp(scores - top), 0.0).astype(bf16).astype(f32)
        total = jnp.sum(weights, axis=0, keepdims=True)
        turned = weights.T
        even = iota((HD, HD), 0) % 2 == 0
        wide = jnp.concatenate(
            [jnp.where(even, turned, 0.0), jnp.where(even, 0.0, turned)], axis=1
        ).astype(bf16)
        values = cv[slots[j]].reshape(256, 512)
        level = jnp.concatenate([top, total], axis=0).astype(bf16)
        for k in range(KVH):
            mixed = jnp.dot(
                wide[32 * k : 32 * k + 32],
                values[:, HD * k : HD * k + HD],
                preferred_element_type=f32,
            )
            for i in range(4):
                for p in range(4):
                    at = 8 * i + 2 * p
                    stat_out[j, 4 * k + i, p] = mixed[at : at + 2].astype(bf16)
                stat_out[j, 4 * k + i, 4] = level

    def send_to(section, partners, kinds, slot):
        for to in partners:
            for source, target, send, receive in kinds:
                pltpu.make_async_remote_copy(
                    source(to),
                    target.at[slot, ten],
                    send.at[slot],
                    receive.at[slot],
                    device_id=(section, to),
                    device_id_type=MESH,
                ).start()

    def send_pages(j, kinds):
        if j < TICKS - 1:

            @pl.when(jnp.logical_not(last))
            def _():
                send_to(following, others + [partner, ten], kinds, j)
        else:
            send_to(sec, others + [partner], kinds, j)

    def stat_pages(j):
        return (lambda to: stat_out.at[j, to], stat_in, stat_send, stat_recv)

    def part_pages(j):
        return (lambda to: part_out.at[j, to // 4], part_in, part_send, part_recv)

    def send_stats(j):
        send_pages(j, [stat_pages(j)])
        if j == TICKS - 1:
            stat_in[j, ten] = stat_out[j, ten]

    def send_parts(j):
        send_pages(j, [part_pages(j)])
        if j == TICKS - 1:
            part_in[j, ten] = part_out[j, ten // 4]

    def wait_bytes(ref, sem):
        pltpu.make_async_copy(ref, ref, sem).wait()

    def arrived(ref, j):
        return ref.at[j] if j < TICKS - 1 else ref.at[j, pl.ds(0, TENSOR - 1)]

    def merge(j):
        wait_bytes(arrived(stat_in, j), stat_recv.at[j])
        for k in range(TENSOR):
            for p in range(4):
                mixed_in[k, 2 * p : 2 * p + 2] = stat_in[j, k, p].astype(f32)
        mixed = mixed_in[...]
        levels = stat_in[j, :, 4].astype(f32)
        tops = levels[:, 0:1, :]
        totals = levels[:, 1:2, :]
        top = jnp.max(tops, axis=0, keepdims=True)
        scale = jnp.exp(tops - top)
        total = jnp.sum(scale * totals, axis=0, keepdims=True)
        share = scale / total
        column = jnp.sum(jnp.where(mine[None], share, 0.0), axis=2, keepdims=True)
        mean = jnp.sum(column * mixed, axis=0)
        level = (top + jnp.log(total))[0]
        return mean, jnp.sum(jnp.where(mine, level, 0.0), axis=1, keepdims=True)

    def arrival(j, level):
        wait_bytes(arrived(part_in, j), part_recv.at[j])
        sums = jnp.sum(part_in[j].astype(f32), axis=0)
        mixture = sums[2:3] + sums[3:4]
        own_col = jnp.sum(jnp.where(mine, mixture, 0.0), axis=1, keepdims=True)
        square_col = jnp.sum(jnp.where(mine_square, mixture, 0.0), axis=1, keepdims=True)
        inverse = lax.rsqrt(square_col / D + EPSILON)
        share = 1.0 / (1.0 + jnp.exp(level - own_col * inverse * HD ** (-0.5)))
        return share, inverse, jnp.where(even_row, sums[0:1], sums[1:2])

    def finish(slot, rows):
        mean, level = merge(slot)
        share, inverse, fresh = arrival(slot, level)
        return rows + (mean + share * (fresh * inverse - mean))

    def project(j, rows, turned=None):
        scaled = features_of(rows * gain8).astype(bf16)
        if turned is None:
            own_part = jnp.dot(scaled, folded[j], preferred_element_type=f32)
        else:
            key_part = jnp.dot(scaled, kw[...], preferred_element_type=f32).astype(bf16)
            own_part = jnp.dot(key_part, turned, preferred_element_type=f32)
        load_wait("vw", j == 0)
        value_part = jnp.dot(scaled, vw[...], preferred_element_type=f32)
        square = rows * rows
        square = square[0:2] + square[2:4] + square[4:6] + square[6:8]
        square = jnp.sum(square, axis=1, keepdims=True)
        write_parts(j, value_part, own_part, square)

    def write_parts(j, values, own, square):
        own_row = jnp.where(even_lane, own[0:1], own[1:2])
        square_row = jnp.where(even_lane, square[0:1], square[1:2])
        for k in range(KVH):
            mixture = jnp.where(lane1 // 32 == k, own_row, square_row)
            high = mixture.astype(bf16).astype(f32)
            part_out[j, k] = jnp.concatenate(
                [values[0:2, HD * k : HD * k + HD], high, mixture - high], axis=0
            ).astype(bf16)

    def blocks(rows):
        return jnp.concatenate(
            [jnp.where(row8 // 2 == h, rows, 0.0) for h in range(4)], axis=1
        ).astype(bf16)

    def over_heads(rows):
        rows = rows + pltpu.roll(rows, 4, 0)
        return rows + pltpu.roll(rows, 2, 0)

    def dots(left, right):
        return jnp.sum(left * right, axis=1, keepdims=True)

    def advance(j):
        row_copy(j - 1).wait_recv()
        rows = row_in[j - 1]
        mean, level = merge(j - 1)
        known = jnp.concatenate([blocks(rows * gain8), blocks(mean * gain8)], axis=0)
        known_value = jnp.dot(known, vw[...], preferred_element_type=f32)
        known_own = jnp.dot(known, folded[j], preferred_element_type=f32)
        rows_rows, rows_mean, mean_mean = dots(rows, rows), dots(rows, mean), dots(mean, mean)
        share, inverse, fresh = arrival(j - 1, level)
        scaled = blocks(fresh * gain8)
        fresh_value = jnp.dot(scaled, vw[...], preferred_element_type=f32)
        fresh_own = jnp.dot(scaled, folded[j], preferred_element_type=f32)
        rest = 1.0 - share
        factor = share * inverse
        square = (
            rows_rows
            + rest * (2.0 * rows_mean + rest * mean_mean)
            + factor * (2.0 * (dots(rows, fresh) + rest * dots(mean, fresh)) + factor * dots(fresh, fresh))
        )
        write_parts(
            j,
            over_heads(known_value[:8] + rest * known_value[8:] + factor * fresh_value),
            over_heads(known_own[:8] + rest * known_own[8:] + factor * fresh_own),
            over_heads(jnp.broadcast_to(square, (8, HD))),
        )
        row_out[j] = (rows + rest * mean + factor * fresh).astype(bf16).astype(f32)

    def load_wait(name, wanted=True):
        if wanted:
            load[name].wait()

    def row_copy(j):
        return pltpu.make_async_remote_copy(
            row_out.at[j],
            row_in.at[j],
            row_send.at[j],
            row_recv.at[j],
            device_id=(following, ten),
            device_id_type=MESH,
        )

    def send_rows(j):
        @pl.when(jnp.logical_not(last))
        def _():
            row_copy(j).start()

    load["q"].wait()
    columns, turned = query_columns(0)
    load["hidden"].wait()
    load["gain"].wait()
    gain8 = heads_of(jnp.broadcast_to(gain_ref[...].astype(f32), (2, 512)))
    rows = heads_of(hidden_ref[...].astype(f32))
    row_out[0] = rows
    load["kw"].wait()
    project(0, rows, turned)
    load["ck"].wait()
    load["cv"].wait()
    stats(0, columns)
    load["entering"].wait()

    @pl.when(first)
    def _():
        pl.semaphore_wait(barrier, 2 * TENSOR - 1)

    @pl.when(jnp.logical_not(jnp.logical_or(first, last)))
    def _():
        pl.semaphore_wait(barrier, TENSOR)

    kinds = [part_pages(0), stat_pages(0)]

    @pl.when(jnp.logical_not(jnp.logical_or(last, alone)))
    def _():
        send_to(following, others + [partner, ten], kinds, 0)
        row_copy(0).start()

    @pl.when(alone)
    def _():
        send_to(sec, others + [partner], kinds, ALONE)
        part_in[ALONE, ten] = part_out[0, ten // 4]
        stat_in[ALONE, ten] = stat_out[0, ten]

    columns, turned = query_columns(1)
    fold(1, turned)
    stats(1, columns)

    @pl.when(alone)
    def _():
        row_out[0] = finish(ALONE, row_out[0]).astype(bf16).astype(f32)
        row_copy(0).start()

    send_stats(1)
    for j in range(1, TICKS):

        @pl.when(first)
        def _():
            rows = heads_of(entering_ref[j - 1].astype(f32))
            row_out[j] = rows
            project(j, rows)

        if j == 1:

            @pl.when(after)
            def _():
                row_copy(0).wait_recv()
                rows = row_in[0]
                row_out[1] = rows
                project(1, rows)

            @pl.when(jnp.logical_not(jnp.logical_or(first, after)))
            def _():
                advance(1)
        else:

            @pl.when(jnp.logical_not(first))
            def _():
                advance(j)

        send_parts(j)
        if j < TICKS - 1:
            send_rows(j)
            columns, turned = query_columns(j + 1)
            fold(j + 1, turned)
            stats(j + 1, columns)
            send_stats(j + 1)
    final = finish(TICKS - 1, row_out[TICKS - 1])
    out_ref[0] = features_of(final).astype(bf16)

    @pl.when(jnp.logical_not(last))
    def _():
        for j in range(TICKS - 1):
            row_copy(j).wait_send()
        for j in range(1, TICKS - 1):
            wait_bytes(part_in.at[j], part_send.at[j])
            wait_bytes(stat_in.at[j], stat_send.at[j])

    @pl.when(jnp.logical_not(jnp.logical_or(last, alone)))
    def _():
        wait_bytes(part_in.at[0], part_send.at[0])
        wait_bytes(stat_in.at[0], stat_send.at[0])

    @pl.when(alone)
    def _():
        wait_bytes(arrived(part_in, ALONE), part_send.at[ALONE])
        wait_bytes(arrived(stat_in, ALONE), stat_send.at[ALONE])

    wait_bytes(arrived(part_in, TICKS - 1), part_send.at[TICKS - 1])
    wait_bytes(arrived(stat_in, TICKS - 1), stat_send.at[TICKS - 1])


def on_device(
    hidden_rows,
    entering_rows,
    norm_gain,
    key_weight,
    value_weight,
    queries,
    cache_keys,
    cache_values,
    lengths,
    plan,
):
    vmem = pl.BlockSpec(memory_space=pltpu.VMEM)
    anywhere = pl.BlockSpec(memory_space=pl.ANY)
    dma = pltpu.SemaphoreType.DMA
    return pl.pallas_call(
        kernel,
        out_shape=pltpu.VMEM((1, 2, 512), bf16),
        in_specs=[anywhere] * 10,
        out_specs=vmem,
        scratch_shapes=[
            pltpu.SMEM((2, 4), jnp.int32),
            pltpu.SMEM((4,), jnp.int32),
            pltpu.VMEM((2, 512), bf16),
            pltpu.VMEM((3, 2, 512), bf16),
            pltpu.VMEM((1, 512), bf16),
            pltpu.VMEM((512, 512), bf16),
            pltpu.VMEM((512, 512), bf16),
            pltpu.VMEM((4, 2, 8192), bf16),
            pltpu.VMEM((4, 2, 128, 512), bf16),
            pltpu.VMEM((4, 2, 128, 512), bf16),
            pltpu.VMEM((128, 128), f32),
            pltpu.VMEM((TICKS, 512, 128), bf16),
            pltpu.VMEM((TICKS, KVH, 4, 128), bf16),
            pltpu.VMEM((TICKS + 1, TENSOR, 4, 128), bf16),
            pltpu.VMEM((TICKS, TENSOR, 5, 2, 128), bf16),
            pltpu.VMEM((TICKS + 1, TENSOR, 5, 2, 128), bf16),
            pltpu.VMEM((TENSOR, 8, 128), f32),
            pltpu.VMEM((TICKS, 8, 128), f32),
            pltpu.VMEM((TICKS - 1, 8, 128), f32),
            dma((10,)),
            dma((TICKS + 1,)),
            dma((TICKS + 1,)),
            dma((TICKS + 1,)),
            dma((TICKS + 1,)),
            dma((TICKS - 1,)),
            dma((TICKS - 1,)),
        ],
        compiler_params=pltpu.CompilerParams(
            collective_id=0, has_side_effects=True, vmem_limit_bytes=60 * 1024 * 1024
        ),
    )(
        hidden_rows,
        entering_rows,
        norm_gain,
        key_weight,
        value_weight,
        queries,
        cache_keys,
        cache_values,
        lengths.T,
        plan,
    )


def solution(mesh):
    in_specs = (
        P("section", None, "tensor"),
        P(None, None, "tensor"),
        P("section", "tensor"),
        P("section", "tensor", None),
        P("section", "tensor", None),
        P("section", None, None, None),
        P("section", None, None, "tensor", None),
        P("section", None, None, "tensor", None),
        P(),
        P(),
    )
    out_specs = P("section", None, "tensor")
    return jax.shard_map(
        on_device, mesh=mesh, in_specs=in_specs, out_specs=out_specs, check_vma=False
    )
```

```python
import functools

import jax
import jax.numpy as jnp
from jax import lax
from jax.experimental import pallas as pl
from jax.experimental.pallas import tpu as pltpu
from jax.sharding import PartitionSpec as P

D = 8192
HQ = 64
KVH = 4
HD = 128
TICKS = 4
TENSOR = 16
EPSILON = 1e-05
SLOW_STEP = 15
ALONE = TICKS
NEG_BIG = -1e30
MESH = pl.DeviceIdType.MESH
f32 = jnp.float32
bf16 = jnp.bfloat16


def iota(shape, axis):
    return lax.broadcasted_iota(jnp.int32, shape, axis)


def block_diagonal(columns):
    group = iota((HD, HD), 1) // 32
    return jnp.concatenate(
        [jnp.where(group == k, columns, 0.0) for k in range(KVH)], axis=0
    ).astype(bf16)


def kernel(
    hidden_hbm,
    entering_hbm,
    gain_hbm,
    kw_hbm,
    vw_hbm,
    q_hbm,
    ck_hbm,
    cv_hbm,
    len_hbm,
    plan_hbm,
    out_ref,
    len_ref,
    plan_ref,
    hidden_ref,
    entering_ref,
    gain_ref,
    kw,
    vw,
    qv,
    ck,
    cv,
    qs,
    folded,
    part_out,
    part_in,
    stat_out,
    stat_in,
    mixed_in,
    row_out,
    row_in,
    load_sem,
    part_send,
    part_recv,
    stat_send,
    stat_recv,
    row_send,
    row_recv,
):
    sections = lax.axis_size("section")
    sec = lax.axis_index("section")
    ten = lax.axis_index("tensor")
    following = lax.rem(sec + 1, sections)
    previous = lax.rem(sec + sections - 1, sections)

    first = sec == 0
    last = sec == sections - 1
    alone = sec == SLOW_STEP
    after = sec == SLOW_STEP + 1
    chip = ten // 2 * 2
    partner = chip + 1 - lax.rem(ten, 2)
    others = [lax.rem(chip + m, TENSOR) for m in (8, 9, 10, 11, 6, 7, 12, 13, 4, 5, 14, 15, 2, 3)]

    barrier = pltpu.get_barrier_semaphore()

    @pl.when(jnp.logical_not(jnp.logical_or(first, after)))
    def _():
        for k in others + [partner, ten]:
            pl.semaphore_signal(barrier, inc=1, device_id=(previous, k), device_id_type=MESH)

    @pl.when(after)
    def _():
        pl.semaphore_signal(barrier, inc=1, device_id=(previous, ten), device_id_type=MESH)

    @pl.when(jnp.logical_or(first, alone))
    def _():
        for k in others + [partner]:
            pl.semaphore_signal(barrier, inc=1, device_id=(sec, k), device_id_type=MESH)

    load = {}
    for i, (name, src, dst) in enumerate(
        [
            ("plan", plan_hbm, plan_ref),
            ("len", len_hbm, len_ref),
            ("q", q_hbm.at[0], qv),
            ("hidden", hidden_hbm.at[0], hidden_ref),
            ("gain", gain_hbm, gain_ref),
            ("kw", kw_hbm.at[0], kw),
            ("ck", ck_hbm.at[0], ck),
            ("vw", vw_hbm.at[0], vw),
            ("cv", cv_hbm.at[0], cv),
            ("entering", entering_hbm, entering_ref),
        ]
    ):
        load[name] = pltpu.make_async_copy(src, dst, load_sem.at[i])
        load[name].start()

    load["plan"].wait()
    load["len"].wait()
    slots = [plan_ref[lax.rem(sec + TICKS - j, TICKS)] for j in range(TICKS)]
    spans = [[len_ref[r, slots[j]] for r in range(2)] for j in range(TICKS)]

    row8 = iota((8, HD), 0)
    lane8 = iota((8, HD), 1)
    even_row = row8 % 2 == 0
    lane1 = iota((1, HD), 1)
    even_lane = lane1 % 2 == 0
    mine = lane8 == row8 + ten * 8
    mine_square = lane8 // 64 == 1 - ten // 8

    def heads_of(block):
        return jnp.concatenate([block[:, h * HD : (h + 1) * HD] for h in range(4)], axis=0)

    def features_of(block):
        return jnp.concatenate([block[2 * h : 2 * h + 2, :] for h in range(4)], axis=1)

    angle_rows = jnp.zeros((8, HD), f32)
    for j in range(TICKS):
        for r in range(2):
            angle_rows = jnp.where(row8 == 2 * j + r, spans[j][r].astype(f32), angle_rows)
    rates = jnp.exp((lane8 % 64).astype(f32) * (-2.0 * jnp.log(f32(500000.0)) / HD))
    angle = angle_rows * rates
    cosines = jnp.cos(angle)
    sines = jnp.sin(angle)
    sines = jnp.where(lane8 < 64, sines, -sines)

    def query_columns(j):
        rows = qv[slots[j]].astype(f32)
        for h in range(HQ):
            qs[2 * h : 2 * h + 2, :] = rows[:, h * HD : (h + 1) * HD]
        q = qs[...]
        cos8 = jnp.concatenate([cosines[2 * j : 2 * j + 2]] * 4, axis=0)
        sin8 = jnp.concatenate([sines[2 * j : 2 * j + 2]] * 4, axis=0)
        other = pltpu.roll(q, 64, 1)
        turned = (
            q.reshape(16, 8, HD) * cos8[None] + other.reshape(16, 8, HD) * sin8[None]
        ).reshape(HD, HD)
        return block_diagonal(q.T), block_diagonal(turned.T)

    def fold(j, turned):
        folded[j] = jnp.dot(kw[...], turned, preferred_element_type=f32).astype(bf16)

    def stats(j, columns):
        keys = ck[slots[j]].reshape(256, 512)
        both = jnp.dot(keys, columns, preferred_element_type=f32)
        scores = jnp.where(even_lane, both[:HD], both[HD:]) * HD ** (-0.5)
        span = jnp.where(even_lane, spans[j][0], spans[j][1])
        valid = iota((HD, HD), 0) + ten * HD < span
        scores = jnp.where(valid, scores, NEG_BIG)
        top = jnp.max(scores, axis=0, keepdims=True).astype(bf16).astype(f32)
        weights = jnp.where(valid, jnp.exp(scores - top), 0.0).astype(bf16).astype(f32)
        total = jnp.sum(weights, axis=0, keepdims=True)
        turned = weights.T
        even = iota((HD, HD), 0) % 2 == 0
        wide = jnp.concatenate(
            [jnp.where(even, turned, 0.0), jnp.where(even, 0.0, turned)], axis=1
        ).astype(bf16)
        values = cv[slots[j]].reshape(256, 512)
        level = jnp.concatenate([top, total], axis=0).astype(bf16)
        for k in range(KVH):
            mixed = jnp.dot(
                wide[32 * k : 32 * k + 32],
                values[:, HD * k : HD * k + HD],
                preferred_element_type=f32,
            )
            for i in range(4):
                for p in range(4):
                    at = 8 * i + 2 * p
                    stat_out[j, 4 * k + i, p] = mixed[at : at + 2].astype(bf16)
                stat_out[j, 4 * k + i, 4] = level

    def send_to(section, partners, kinds, slot):
        for to in partners:
            for source, target, send, receive in kinds:
                pltpu.make_async_remote_copy(
                    source(to),
                    target.at[slot, ten],
                    send.at[slot],
                    receive.at[slot],
                    device_id=(section, to),
                    device_id_type=MESH,
                ).start()

    def send_pages(j, kinds):
        if j < TICKS - 1:

            @pl.when(jnp.logical_not(last))
            def _():
                send_to(following, others + [partner, ten], kinds, j)
        else:
            send_to(sec, others + [partner], kinds, j)

    def stat_pages(j):
        return (lambda to: stat_out.at[j, to], stat_in, stat_send, stat_recv)

    def part_pages(j):
        return (lambda to: part_out.at[j, to // 4], part_in, part_send, part_recv)

    def send_stats(j):
        send_pages(j, [stat_pages(j)])
        if j == TICKS - 1:
            stat_in[j, ten] = stat_out[j, ten]

    def send_parts(j):
        send_pages(j, [part_pages(j)])
        if j == TICKS - 1:
            part_in[j, ten] = part_out[j, ten // 4]

    def wait_bytes(ref, sem):
        pltpu.make_async_copy(ref, ref, sem).wait()

    def arrived(ref, j):
        return ref.at[j] if j < TICKS - 1 else ref.at[j, pl.ds(0, TENSOR - 1)]

    def merge(j):
        wait_bytes(arrived(stat_in, j), stat_recv.at[j])
        for k in range(TENSOR):
            for p in range(4):
                mixed_in[k, 2 * p : 2 * p + 2] = stat_in[j, k, p].astype(f32)
        mixed = mixed_in[...]
        levels = stat_in[j, :, 4].astype(f32)
        tops = levels[:, 0:1, :]
        totals = levels[:, 1:2, :]
        top = jnp.max(tops, axis=0, keepdims=True)
        scale = jnp.exp(tops - top)
        total = jnp.sum(scale * totals, axis=0, keepdims=True)
        share = scale / total
        column = jnp.sum(jnp.where(mine[None], share, 0.0), axis=2, keepdims=True)
        mean = jnp.sum(column * mixed, axis=0)
        level = (top + jnp.log(total))[0]
        return mean, jnp.sum(jnp.where(mine, level, 0.0), axis=1, keepdims=True)

    def arrival(j, level):
        wait_bytes(arrived(part_in, j), part_recv.at[j])
        sums = jnp.sum(part_in[j].astype(f32), axis=0)
        mixture = sums[2:3] + sums[3:4]
        own_col = jnp.sum(jnp.where(mine, mixture, 0.0), axis=1, keepdims=True)
        squares = jnp.where(even_row, sums[2:3], sums[3:4])
        square_col = jnp.sum(jnp.where(mine_square, squares, 0.0), axis=1, keepdims=True)
        inverse = lax.rsqrt(square_col / D + EPSILON)
        share = 1.0 / (1.0 + jnp.exp(level - own_col * inverse * HD ** (-0.5)))
        return share, inverse, jnp.where(even_row, sums[0:1], sums[1:2])

    def finish(slot, rows):
        mean, level = merge(slot)
        share, inverse, fresh = arrival(slot, level)
        return rows + (mean + share * (fresh * inverse - mean))

    def project(j, rows, turned=None):
        scaled = features_of(rows * gain8).astype(bf16)
        if turned is None:
            own_part = jnp.dot(scaled, folded[j], preferred_element_type=f32)
        else:
            key_part = jnp.dot(scaled, kw[...], preferred_element_type=f32).astype(bf16)
            own_part = jnp.dot(key_part, turned, preferred_element_type=f32)
        load_wait("vw", j == 0)
        value_part = jnp.dot(scaled, vw[...], preferred_element_type=f32)
        write_parts(j, value_part, own_part, over_heads(rows * rows))

    def write_parts(j, values, own, squares):
        own_row = jnp.where(even_lane, own[0:1], own[1:2])
        high = own_row.astype(bf16).astype(f32)
        low = own_row - high
        squares = squares + pltpu.roll(squares, 64, 1)
        for k in range(KVH):
            here = lane1 // 32 == k
            there = lane1 // 64 == 1 - k // 2
            part_out[j, k] = jnp.concatenate(
                [
                    values[0:2, HD * k : HD * k + HD],
                    jnp.where(here, high, jnp.where(there, squares[0:1], 0.0)),
                    jnp.where(here, low, jnp.where(there, squares[1:2], 0.0)),
                ],
                axis=0,
            ).astype(bf16)

    def blocks(rows):
        return jnp.concatenate(
            [jnp.where(row8 // 2 == h, rows, 0.0) for h in range(4)], axis=1
        ).astype(bf16)

    def over_heads(rows):
        rows = rows + pltpu.roll(rows, 4, 0)
        return rows + pltpu.roll(rows, 2, 0)

    def advance(j):
        row_copy(j - 1).wait_recv()
        rows = row_in[j - 1]
        mean, level = merge(j - 1)
        known = jnp.concatenate([blocks(rows * gain8), blocks(mean * gain8)], axis=0)
        known_value = jnp.dot(known, vw[...], preferred_element_type=f32)
        known_own = jnp.dot(known, folded[j], preferred_element_type=f32)
        share, inverse, fresh = arrival(j - 1, level)
        scaled = blocks(fresh * gain8)
        fresh_value = jnp.dot(scaled, vw[...], preferred_element_type=f32)
        fresh_own = jnp.dot(scaled, folded[j], preferred_element_type=f32)
        rest = 1.0 - share
        factor = share * inverse
        rows = rows + rest * mean + factor * fresh
        write_parts(
            j,
            over_heads(known_value[:8] + rest * known_value[8:] + factor * fresh_value),
            over_heads(known_own[:8] + rest * known_own[8:] + factor * fresh_own),
            over_heads(rows * rows),
        )
        row_out[j] = rows.astype(bf16).astype(f32)

    def load_wait(name, wanted=True):
        if wanted:
            load[name].wait()

    def row_copy(j):
        return pltpu.make_async_remote_copy(
            row_out.at[j],
            row_in.at[j],
            row_send.at[j],
            row_recv.at[j],
            device_id=(following, ten),
            device_id_type=MESH,
        )

    def send_rows(j):
        @pl.when(jnp.logical_not(last))
        def _():
            row_copy(j).start()

    load["q"].wait()
    columns, turned = query_columns(0)
    load["hidden"].wait()
    load["gain"].wait()
    gain8 = heads_of(jnp.broadcast_to(gain_ref[...].astype(f32), (2, 512)))
    rows = heads_of(hidden_ref[...].astype(f32))
    row_out[0] = rows
    load["kw"].wait()
    project(0, rows, turned)
    load["ck"].wait()
    load["cv"].wait()
    stats(0, columns)
    load["entering"].wait()

    @pl.when(first)
    def _():
        pl.semaphore_wait(barrier, 2 * TENSOR - 1)

    @pl.when(jnp.logical_not(jnp.logical_or(first, last)))
    def _():
        pl.semaphore_wait(barrier, TENSOR)

    kinds = [part_pages(0), stat_pages(0)]

    @pl.when(jnp.logical_not(jnp.logical_or(last, alone)))
    def _():
        send_to(following, others + [partner, ten], kinds, 0)
        row_copy(0).start()

    @pl.when(alone)
    def _():
        send_to(sec, others + [partner], kinds, ALONE)
        part_in[ALONE, ten] = part_out[0, ten // 4]
        stat_in[ALONE, ten] = stat_out[0, ten]

    columns, turned = query_columns(1)
    fold(1, turned)
    stats(1, columns)

    @pl.when(alone)
    def _():
        row_out[0] = finish(ALONE, row_out[0]).astype(bf16).astype(f32)
        row_copy(0).start()

    send_stats(1)
    for j in range(1, TICKS):

        @pl.when(first)
        def _():
            rows = heads_of(entering_ref[j - 1].astype(f32))
            row_out[j] = rows
            project(j, rows)

        if j == 1:

            @pl.when(after)
            def _():
                row_copy(0).wait_recv()
                rows = row_in[0]
                row_out[1] = rows
                project(1, rows)

            @pl.when(jnp.logical_not(jnp.logical_or(first, after)))
            def _():
                advance(1)
        else:

            @pl.when(jnp.logical_not(first))
            def _():
                advance(j)

        send_parts(j)
        if j < TICKS - 1:
            send_rows(j)
            columns, turned = query_columns(j + 1)
            fold(j + 1, turned)
            stats(j + 1, columns)
            send_stats(j + 1)
    final = finish(TICKS - 1, row_out[TICKS - 1])
    out_ref[0] = features_of(final).astype(bf16)

    @pl.when(jnp.logical_not(last))
    def _():
        for j in range(TICKS - 1):
            row_copy(j).wait_send()
        for j in range(1, TICKS - 1):
            wait_bytes(part_in.at[j], part_send.at[j])
            wait_bytes(stat_in.at[j], stat_send.at[j])

    @pl.when(jnp.logical_not(jnp.logical_or(last, alone)))
    def _():
        wait_bytes(part_in.at[0], part_send.at[0])
        wait_bytes(stat_in.at[0], stat_send.at[0])

    @pl.when(alone)
    def _():
        wait_bytes(arrived(part_in, ALONE), part_send.at[ALONE])
        wait_bytes(arrived(stat_in, ALONE), stat_send.at[ALONE])

    wait_bytes(arrived(part_in, TICKS - 1), part_send.at[TICKS - 1])
    wait_bytes(arrived(stat_in, TICKS - 1), stat_send.at[TICKS - 1])


def on_device(
    hidden_rows,
    entering_rows,
    norm_gain,
    key_weight,
    value_weight,
    queries,
    cache_keys,
    cache_values,
    lengths,
    plan,
):
    vmem = pl.BlockSpec(memory_space=pltpu.VMEM)
    anywhere = pl.BlockSpec(memory_space=pl.ANY)
    dma = pltpu.SemaphoreType.DMA
    return pl.pallas_call(
        kernel,
        out_shape=pltpu.VMEM((1, 2, 512), bf16),
        in_specs=[anywhere] * 10,
        out_specs=vmem,
        scratch_shapes=[
            pltpu.SMEM((2, 4), jnp.int32),
            pltpu.SMEM((4,), jnp.int32),
            pltpu.VMEM((2, 512), bf16),
            pltpu.VMEM((3, 2, 512), bf16),
            pltpu.VMEM((1, 512), bf16),
            pltpu.VMEM((512, 512), bf16),
            pltpu.VMEM((512, 512), bf16),
            pltpu.VMEM((4, 2, 8192), bf16),
            pltpu.VMEM((4, 2, 128, 512), bf16),
            pltpu.VMEM((4, 2, 128, 512), bf16),
            pltpu.VMEM((128, 128), f32),
            pltpu.VMEM((TICKS, 512, 128), bf16),
            pltpu.VMEM((TICKS, KVH, 4, 128), bf16),
            pltpu.VMEM((TICKS + 1, TENSOR, 4, 128), bf16),
            pltpu.VMEM((TICKS, TENSOR, 5, 2, 128), bf16),
            pltpu.VMEM((TICKS + 1, TENSOR, 5, 2, 128), bf16),
            pltpu.VMEM((TENSOR, 8, 128), f32),
            pltpu.VMEM((TICKS, 8, 128), f32),
            pltpu.VMEM((TICKS - 1, 8, 128), f32),
            dma((10,)),
            dma((TICKS + 1,)),
            dma((TICKS + 1,)),
            dma((TICKS + 1,)),
            dma((TICKS + 1,)),
            dma((TICKS - 1,)),
            dma((TICKS - 1,)),
        ],
        compiler_params=pltpu.CompilerParams(
            collective_id=0, has_side_effects=True, vmem_limit_bytes=60 * 1024 * 1024
        ),
    )(
        hidden_rows,
        entering_rows,
        norm_gain,
        key_weight,
        value_weight,
        queries,
        cache_keys,
        cache_values,
        lengths.T,
        plan,
    )


def solution(mesh):
    in_specs = (
        P("section", None, "tensor"),
        P(None, None, "tensor"),
        P("section", "tensor"),
        P("section", "tensor", None),
        P("section", "tensor", None),
        P("section", None, None, None),
        P("section", None, None, "tensor", None),
        P("section", None, None, "tensor", None),
        P(),
        P(),
    )
    out_specs = P("section", None, "tensor")
    return jax.shard_map(
        on_device, mesh=mesh, in_specs=in_specs, out_specs=out_specs, check_vma=False
    )
```

```python
import functools

import jax
import jax.numpy as jnp
from jax import lax
from jax.experimental import pallas as pl
from jax.experimental.pallas import tpu as pltpu
from jax.sharding import PartitionSpec as P

D = 8192
HQ = 64
KVH = 4
HD = 128
TICKS = 4
TENSOR = 16
EPSILON = 1e-05
SLOW_STEP = 15
ALONE = TICKS
NEG_BIG = -1e30
MESH = pl.DeviceIdType.MESH
f32 = jnp.float32
bf16 = jnp.bfloat16


def iota(shape, axis):
    return lax.broadcasted_iota(jnp.int32, shape, axis)


def block_diagonal(columns):
    group = iota((HD, HD), 1) // 32
    return jnp.concatenate(
        [jnp.where(group == k, columns, 0.0) for k in range(KVH)], axis=0
    ).astype(bf16)


def kernel(
    hidden_hbm,
    entering_hbm,
    gain_hbm,
    kw_hbm,
    vw_hbm,
    q_hbm,
    ck_hbm,
    cv_hbm,
    len_hbm,
    plan_hbm,
    out_ref,
    len_ref,
    plan_ref,
    hidden_ref,
    entering_ref,
    gain_ref,
    kw,
    vw,
    qv,
    ck,
    cv,
    qs,
    folded,
    part_out,
    part_in,
    stat_out,
    stat_in,
    mixed_in,
    row_out,
    row_in,
    load_sem,
    part_send,
    part_recv,
    stat_send,
    stat_recv,
    row_send,
    row_recv,
):
    sections = lax.axis_size("section")
    sec = lax.axis_index("section")
    ten = lax.axis_index("tensor")
    following = lax.rem(sec + 1, sections)
    previous = lax.rem(sec + sections - 1, sections)

    first = sec == 0
    last = sec == sections - 1
    alone = sec == SLOW_STEP
    after = sec == SLOW_STEP + 1
    chip = ten // 2 * 2
    partner = chip + 1 - lax.rem(ten, 2)
    others = [lax.rem(chip + m, TENSOR) for m in (8, 9, 10, 11, 6, 7, 12, 13, 4, 5, 14, 15, 2, 3)]

    barrier = pltpu.get_barrier_semaphore()

    @pl.when(jnp.logical_not(jnp.logical_or(first, after)))
    def _():
        for k in others + [partner, ten]:
            pl.semaphore_signal(barrier, inc=1, device_id=(previous, k), device_id_type=MESH)

    @pl.when(after)
    def _():
        pl.semaphore_signal(barrier, inc=1, device_id=(previous, ten), device_id_type=MESH)

    @pl.when(jnp.logical_or(first, alone))
    def _():
        for k in others + [partner]:
            pl.semaphore_signal(barrier, inc=1, device_id=(sec, k), device_id_type=MESH)

    load = {}
    for i, (name, src, dst) in enumerate(
        [
            ("plan", plan_hbm, plan_ref),
            ("len", len_hbm, len_ref),
            ("q", q_hbm.at[0], qv),
            ("hidden", hidden_hbm.at[0], hidden_ref),
            ("gain", gain_hbm, gain_ref),
            ("kw", kw_hbm.at[0], kw),
            ("ck", ck_hbm.at[0], ck),
            ("vw", vw_hbm.at[0], vw),
            ("cv", cv_hbm.at[0], cv),
            ("entering", entering_hbm, entering_ref),
        ]
    ):
        load[name] = pltpu.make_async_copy(src, dst, load_sem.at[i])
        load[name].start()

    load["plan"].wait()
    load["len"].wait()
    slots = [plan_ref[lax.rem(sec + TICKS - j, TICKS)] for j in range(TICKS)]
    spans = [[len_ref[r, slots[j]] for r in range(2)] for j in range(TICKS)]

    row8 = iota((8, HD), 0)
    lane8 = iota((8, HD), 1)
    even_row = row8 % 2 == 0
    lane1 = iota((1, HD), 1)
    even_lane = lane1 % 2 == 0
    mine = lane8 == row8 + ten * 8
    mine_square = lane8 == lax.rem(row8 + ten * 8 + 64, HD)

    def heads_of(block):
        return jnp.concatenate([block[:, h * HD : (h + 1) * HD] for h in range(4)], axis=0)

    def features_of(block):
        return jnp.concatenate([block[2 * h : 2 * h + 2, :] for h in range(4)], axis=1)

    angle_rows = jnp.zeros((8, HD), f32)
    for j in range(TICKS):
        for r in range(2):
            angle_rows = jnp.where(row8 == 2 * j + r, spans[j][r].astype(f32), angle_rows)
    rates = jnp.exp((lane8 % 64).astype(f32) * (-2.0 * jnp.log(f32(500000.0)) / HD))
    angle = angle_rows * rates
    cosines = jnp.cos(angle)
    sines = jnp.sin(angle)
    sines = jnp.where(lane8 < 64, sines, -sines)

    def query_columns(j):
        rows = qv[slots[j]].astype(f32)
        for h in range(HQ):
            qs[2 * h : 2 * h + 2, :] = rows[:, h * HD : (h + 1) * HD]
        q = qs[...]
        cos8 = jnp.concatenate([cosines[2 * j : 2 * j + 2]] * 4, axis=0)
        sin8 = jnp.concatenate([sines[2 * j : 2 * j + 2]] * 4, axis=0)
        other = pltpu.roll(q, 64, 1)
        turned = (
            q.reshape(16, 8, HD) * cos8[None] + other.reshape(16, 8, HD) * sin8[None]
        ).reshape(HD, HD)
        return block_diagonal(q.T), block_diagonal(turned.T)

    def fold(j, turned):
        folded[j] = jnp.dot(kw[...], turned, preferred_element_type=f32).astype(bf16)

    def stats(j, columns):
        keys = ck[slots[j]].reshape(256, 512)
        both = jnp.dot(keys, columns, preferred_element_type=f32)
        scores = jnp.where(even_lane, both[:HD], both[HD:]) * HD ** (-0.5)
        span = jnp.where(even_lane, spans[j][0], spans[j][1])
        valid = iota((HD, HD), 0) + ten * HD < span
        scores = jnp.where(valid, scores, NEG_BIG)
        top = jnp.max(scores, axis=0, keepdims=True).astype(bf16).astype(f32)
        weights = jnp.where(valid, jnp.exp(scores - top), 0.0).astype(bf16).astype(f32)
        total = jnp.sum(weights, axis=0, keepdims=True)
        turned = weights.T
        even = iota((HD, HD), 0) % 2 == 0
        wide = jnp.concatenate(
            [jnp.where(even, turned, 0.0), jnp.where(even, 0.0, turned)], axis=1
        ).astype(bf16)
        values = cv[slots[j]].reshape(256, 512)
        level = jnp.concatenate([top, total], axis=0).astype(bf16)
        for k in range(KVH):
            mixed = jnp.dot(
                wide[32 * k : 32 * k + 32],
                values[:, HD * k : HD * k + HD],
                preferred_element_type=f32,
            )
            for i in range(4):
                for p in range(4):
                    at = 8 * i + 2 * p
                    stat_out[j, 4 * k + i, p] = mixed[at : at + 2].astype(bf16)
                stat_out[j, 4 * k + i, 4] = level

    def send_to(section, partners, kinds, slot):
        for to in partners:
            for source, target, send, receive in kinds:
                pltpu.make_async_remote_copy(
                    source(to),
                    target.at[slot, ten],
                    send.at[slot],
                    receive.at[slot],
                    device_id=(section, to),
                    device_id_type=MESH,
                ).start()

    def send_pages(j, kinds):
        if j < TICKS - 1:

            @pl.when(jnp.logical_not(last))
            def _():
                send_to(following, others + [partner, ten], kinds, j)
        else:
            send_to(sec, others + [partner], kinds, j)

    def stat_pages(j):
        return (lambda to: stat_out.at[j, to], stat_in, stat_send, stat_recv)

    def part_pages(j):
        return (lambda to: part_out.at[j, to // 4], part_in, part_send, part_recv)

    def send_stats(j):
        send_pages(j, [stat_pages(j)])
        if j == TICKS - 1:
            stat_in[j, ten] = stat_out[j, ten]

    def send_parts(j):
        send_pages(j, [part_pages(j)])
        if j == TICKS - 1:
            part_in[j, ten] = part_out[j, ten // 4]

    def wait_bytes(ref, sem):
        pltpu.make_async_copy(ref, ref, sem).wait()

    def arrived(ref, j):
        return ref.at[j] if j < TICKS - 1 else ref.at[j, pl.ds(0, TENSOR - 1)]

    def merge(j):
        wait_bytes(arrived(stat_in, j), stat_recv.at[j])
        for k in range(TENSOR):
            for p in range(4):
                mixed_in[k, 2 * p : 2 * p + 2] = stat_in[j, k, p].astype(f32)
        mixed = mixed_in[...]
        levels = stat_in[j, :, 4].astype(f32)
        tops = levels[:, 0:1, :]
        totals = levels[:, 1:2, :]
        top = jnp.max(tops, axis=0, keepdims=True)
        scale = jnp.exp(tops - top)
        total = jnp.sum(scale * totals, axis=0, keepdims=True)
        share = scale / total
        column = jnp.sum(jnp.where(mine[None], share, 0.0), axis=2, keepdims=True)
        mean = jnp.sum(column * mixed, axis=0)
        level = (top + jnp.log(total))[0]
        return mean, jnp.sum(jnp.where(mine, level, 0.0), axis=1, keepdims=True)

    def arrival(j, level):
        wait_bytes(arrived(part_in, j), part_recv.at[j])
        sums = jnp.sum(part_in[j].astype(f32), axis=0)
        mixture = sums[2:3] + sums[3:4]
        own_col = jnp.sum(jnp.where(mine, mixture, 0.0), axis=1, keepdims=True)
        square_col = jnp.sum(jnp.where(mine_square, mixture, 0.0), axis=1, keepdims=True)
        inverse = lax.rsqrt(square_col / D + EPSILON)
        share = 1.0 / (1.0 + jnp.exp(level - own_col * inverse * HD ** (-0.5)))
        return share, inverse, jnp.where(even_row, sums[0:1], sums[1:2])

    def finish(slot, rows):
        mean, level = merge(slot)
        share, inverse, fresh = arrival(slot, level)
        return rows + (mean + share * (fresh * inverse - mean))

    def project(j, rows, turned=None):
        scaled = features_of(rows * gain8).astype(bf16)
        if turned is None:
            own_part = jnp.dot(scaled, folded[j], preferred_element_type=f32)
        else:
            key_part = jnp.dot(scaled, kw[...], preferred_element_type=f32).astype(bf16)
            own_part = jnp.dot(key_part, turned, preferred_element_type=f32)
        load_wait("vw", j == 0)
        value_part = jnp.dot(scaled, vw[...], preferred_element_type=f32)
        square = rows * rows
        square = square[0:2] + square[2:4] + square[4:6] + square[6:8]
        square = jnp.sum(square, axis=1, keepdims=True)
        write_parts(j, value_part, own_part, square)

    def write_parts(j, values, own, square):
        own_row = jnp.where(even_lane, own[0:1], own[1:2])
        square_row = jnp.where(even_lane, square[0:1], square[1:2])
        for k in range(KVH):
            mixture = jnp.where(lane1 // 32 == k, own_row, square_row)
            high = mixture.astype(bf16).astype(f32)
            part_out[j, k] = jnp.concatenate(
                [values[0:2, HD * k : HD * k + HD], high, mixture - high], axis=0
            ).astype(bf16)

    def blocks(rows):
        return jnp.concatenate(
            [jnp.where(row8 // 2 == h, rows, 0.0) for h in range(4)], axis=1
        ).astype(bf16)

    def over_heads(rows):
        rows = rows + pltpu.roll(rows, 4, 0)
        return rows + pltpu.roll(rows, 2, 0)

    def dots(left, right):
        return jnp.sum(left * right, axis=1, keepdims=True)

    def advance(j):
        row_copy(j - 1).wait_recv()
        rows = row_in[j - 1]
        mean, level = merge(j - 1)
        known = jnp.concatenate([blocks(rows * gain8), blocks(mean * gain8)], axis=0)
        known_value = jnp.dot(known, vw[...], preferred_element_type=f32)
        known_own = jnp.dot(known, folded[j], preferred_element_type=f32)
        rows_rows, rows_mean, mean_mean = dots(rows, rows), dots(rows, mean), dots(mean, mean)
        share, inverse, fresh = arrival(j - 1, level)
        scaled = blocks(fresh * gain8)
        fresh_value = jnp.dot(scaled, vw[...], preferred_element_type=f32)
        fresh_own = jnp.dot(scaled, folded[j], preferred_element_type=f32)
        rest = 1.0 - share
        factor = share * inverse
        square = (
            rows_rows
            + rest * (2.0 * rows_mean + rest * mean_mean)
            + factor * (2.0 * (dots(rows, fresh) + rest * dots(mean, fresh)) + factor * dots(fresh, fresh))
        )
        write_parts(
            j,
            over_heads(known_value[:8] + rest * known_value[8:] + factor * fresh_value),
            over_heads(known_own[:8] + rest * known_own[8:] + factor * fresh_own),
            over_heads(jnp.broadcast_to(square, (8, HD))),
        )
        row_out[j] = (rows + rest * mean + factor * fresh).astype(bf16).astype(f32)

    def load_wait(name, wanted=True):
        if wanted:
            load[name].wait()

    def row_copy(j):
        return pltpu.make_async_remote_copy(
            row_out.at[j],
            row_in.at[j],
            row_send.at[j],
            row_recv.at[j],
            device_id=(following, ten),
            device_id_type=MESH,
        )

    def send_rows(j):
        @pl.when(jnp.logical_not(last))
        def _():
            row_copy(j).start()

    load["q"].wait()
    columns, turned = query_columns(0)
    load["hidden"].wait()
    load["gain"].wait()
    gain8 = heads_of(jnp.broadcast_to(gain_ref[...].astype(f32), (2, 512)))
    rows = heads_of(hidden_ref[...].astype(f32))
    row_out[0] = rows
    load["kw"].wait()
    project(0, rows, turned)
    load["ck"].wait()
    load["cv"].wait()
    stats(0, columns)
    load["entering"].wait()

    @pl.when(first)
    def _():
        pl.semaphore_wait(barrier, 2 * TENSOR - 1)

    @pl.when(jnp.logical_not(jnp.logical_or(first, last)))
    def _():
        pl.semaphore_wait(barrier, TENSOR)

    kinds = [part_pages(0), stat_pages(0)]

    @pl.when(jnp.logical_not(jnp.logical_or(last, alone)))
    def _():
        send_to(following, others + [partner, ten], kinds, 0)
        row_copy(0).start()

    @pl.when(alone)
    def _():
        send_to(sec, others + [partner], kinds, ALONE)
        part_in[ALONE, ten] = part_out[0, ten // 4]
        stat_in[ALONE, ten] = stat_out[0, ten]

    columns, turned = query_columns(1)
    fold(1, turned)
    stats(1, columns)

    @pl.when(alone)
    def _():
        row_out[0] = finish(ALONE, row_out[0]).astype(bf16).astype(f32)
        row_copy(0).start()

    send_stats(1)
    for j in range(1, TICKS):

        @pl.when(first)
        def _():
            rows = heads_of(entering_ref[j - 1].astype(f32))
            row_out[j] = rows
            project(j, rows)

        if j == 1:

            @pl.when(after)
            def _():
                row_copy(0).wait_recv()
                rows = row_in[0]
                row_out[1] = rows
                project(1, rows)

            @pl.when(jnp.logical_not(jnp.logical_or(first, after)))
            def _():
                advance(1)
        else:

            @pl.when(jnp.logical_not(first))
            def _():
                advance(j)

        send_parts(j)
        if j < TICKS - 1:
            send_rows(j)
            columns, turned = query_columns(j + 1)
            fold(j + 1, turned)
            stats(j + 1, columns)
            send_stats(j + 1)
    final = finish(TICKS - 1, row_out[TICKS - 1])
    out_ref[0] = features_of(final).astype(bf16)

    @pl.when(jnp.logical_not(last))
    def _():
        for j in range(TICKS - 1):
            row_copy(j).wait_send()
        for j in range(1, TICKS - 1):
            wait_bytes(part_in.at[j], part_send.at[j])
            wait_bytes(stat_in.at[j], stat_send.at[j])

    @pl.when(jnp.logical_not(jnp.logical_or(last, alone)))
    def _():
        wait_bytes(part_in.at[0], part_send.at[0])
        wait_bytes(stat_in.at[0], stat_send.at[0])

    @pl.when(alone)
    def _():
        wait_bytes(arrived(part_in, ALONE), part_send.at[ALONE])
        wait_bytes(arrived(stat_in, ALONE), stat_send.at[ALONE])

    wait_bytes(arrived(part_in, TICKS - 1), part_send.at[TICKS - 1])
    wait_bytes(arrived(stat_in, TICKS - 1), stat_send.at[TICKS - 1])


def on_device(
    hidden_rows,
    entering_rows,
    norm_gain,
    key_weight,
    value_weight,
    queries,
    cache_keys,
    cache_values,
    lengths,
    plan,
):
    vmem = pl.BlockSpec(memory_space=pltpu.VMEM)
    anywhere = pl.BlockSpec(memory_space=pl.ANY)
    dma = pltpu.SemaphoreType.DMA
    return pl.pallas_call(
        kernel,
        out_shape=pltpu.VMEM((1, 2, 512), bf16),
        in_specs=[anywhere] * 10,
        out_specs=vmem,
        scratch_shapes=[
            pltpu.SMEM((2, 4), jnp.int32),
            pltpu.SMEM((4,), jnp.int32),
            pltpu.VMEM((2, 512), bf16),
            pltpu.VMEM((3, 2, 512), bf16),
            pltpu.VMEM((1, 512), bf16),
            pltpu.VMEM((512, 512), bf16),
            pltpu.VMEM((512, 512), bf16),
            pltpu.VMEM((4, 2, 8192), bf16),
            pltpu.VMEM((4, 2, 128, 512), bf16),
            pltpu.VMEM((4, 2, 128, 512), bf16),
            pltpu.VMEM((128, 128), f32),
            pltpu.VMEM((TICKS, 512, 128), bf16),
            pltpu.VMEM((TICKS, KVH, 4, 128), bf16),
            pltpu.VMEM((TICKS + 1, TENSOR, 4, 128), bf16),
            pltpu.VMEM((TICKS, TENSOR, 5, 2, 128), bf16),
            pltpu.VMEM((TICKS + 1, TENSOR, 5, 2, 128), bf16),
            pltpu.VMEM((TENSOR, 8, 128), f32),
            pltpu.VMEM((TICKS, 8, 128), f32),
            pltpu.VMEM((TICKS - 1, 8, 128), f32),
            dma((10,)),
            dma((TICKS + 1,)),
            dma((TICKS + 1,)),
            dma((TICKS + 1,)),
            dma((TICKS + 1,)),
            dma((TICKS - 1,)),
            dma((TICKS - 1,)),
        ],
        compiler_params=pltpu.CompilerParams(
            collective_id=0, has_side_effects=True, vmem_limit_bytes=60 * 1024 * 1024
        ),
    )(
        hidden_rows,
        entering_rows,
        norm_gain,
        key_weight,
        value_weight,
        queries,
        cache_keys,
        cache_values,
        lengths.T,
        plan,
    )


def solution(mesh):
    in_specs = (
        P("section", None, "tensor"),
        P(None, None, "tensor"),
        P("section", "tensor"),
        P("section", "tensor", None),
        P("section", "tensor", None),
        P("section", None, None, None),
        P("section", None, None, "tensor", None),
        P("section", None, None, "tensor", None),
        P(),
        P(),
    )
    out_specs = P("section", None, "tensor")
    return jax.shard_map(
        on_device, mesh=mesh, in_specs=in_specs, out_specs=out_specs, check_vma=False
    )
```
